256 devices in a mesh: virt: 64 (over z, y, core), rep: 4 (over x).
Axes of the slice: x: 4, y: 4, z: 8, core: 2. Of those that a mesh axis runs over, the one named last changes fastest.
Arguments:
- t2_packed: float32 [256, 921600], P(None, ('virt', 'rep')), may hold values from -6 to 6
- w_packed: float32 [921600, 512], P(('virt', 'rep')), may hold values from -0.015625 to 0.015625
- pair_list: int32 [2, 921600], P(None, ('virt', 'rep')), may hold values from 0 to 959, as said below
- block_starts: int32 [8], replicated, may hold values from 0 to 921599, as said below
- singles: float32 [120, 960], replicated, may hold values from -3 to 3
- row_pairs: int32 [8, 256, 2], replicated, may hold values from 0 to 119, as said below
- col_pairs: int32 [8, 512, 2], P(None, 'rep'), may hold values from 0 to 959, as said below
- t2_slab: float32 [8, 256, 512], P(None, 'virt', 'rep'), may hold values from -6 to 6
- w_hole: float32 [8, 256, 256], P(None, 'virt'), may hold values from -0.375 to 0.375
- driver: float32 [8, 256, 512], P(None, 'virt', 'rep'), may hold values from -6 to 6
- occ_energy: float32 [120], replicated, may hold values from -2 to -0.5
- vir_energy: float32 [960], replicated, may hold values from 0.2 to 3
Outputs:
- t2_new: float32 [8, 256, 512], P(None, 'virt', 'rep')
The draws below stay inside these ranges and needn't reach their ends.
Inputs may be any that keep to these rules, and one draw needn't show every extreme that they name: Column p of pair_list holds the two virtual orbitals of packed pair p; every ordered pair of virtual orbitals occurs once, grouped into irrep blocks that begin at block_starts. block_starts[0] is 0 and the starts rise; every block holds at least 28800 pairs. `row_pairs`: the irreps of the two occupied orbitals of a slot of group h multiply to h. `col_pairs`: the irreps of the two virtual orbitals of a slab pair of group h multiply to h.
All inputs are finite; a program needn't handle non-finite values.
Results may differ from the reference program's by a relative error of at most 0.0003.
Values sent between devices are 32-bit elements; how exact they have to be, the bound alone decides.
A program may use at most 128 MiB of HBM per device.

```python
import jax
import jax.numpy as jnp
from jax import lax

O = 120
V = 960
GROUPS = 8
RB = 256
CB = 512
NCD = 921600
N_VIRT = 64
N_REP = 4


def virt_labels(key):
    fixed_part = jnp.arange(V // 2, dtype=jnp.int32) % 8
    random_part = jax.random.randint(jax.random.fold_in(key, 101), (V - V // 2,), 0, 8, dtype=jnp.int32)
    return jax.random.permutation(jax.random.fold_in(key, 102), jnp.concatenate([fixed_part, random_part]))


def pair_blocks(labels):
    positions = jnp.arange(NCD, dtype=jnp.int32)
    return jnp.bitwise_xor(labels[positions // V], labels[positions % V])


def partner_pairs(key, labels, count, slots):
    ordering = jnp.argsort(labels * count + jnp.arange(count, dtype=jnp.int32)).astype(jnp.int32)
    block_sizes = jnp.sum((labels[:, None] == jnp.arange(8, dtype=jnp.int32)[None, :]).astype(jnp.int32), axis=0)
    starts = jnp.concatenate([jnp.zeros((1,), jnp.int32), jnp.cumsum(block_sizes)[:7].astype(jnp.int32)])
    first_orbit = jax.random.randint(jax.random.fold_in(key, 1), (8, slots), 0, count, dtype=jnp.int32)
    target = jnp.bitwise_xor(labels[first_orbit], jnp.arange(8, dtype=jnp.int32)[:, None])
    chosen = jax.random.randint(jax.random.fold_in(key, 2), (8, slots), 0, block_sizes[target], dtype=jnp.int32)
    second = ordering[starts[target] + chosen]
    return jnp.stack([first_orbit, second], axis=2).astype(jnp.int32)


def draw_pair_list(key, part):
    blocks = pair_blocks(virt_labels(key))
    ordering = jnp.argsort(blocks * NCD + jnp.arange(NCD, dtype=jnp.int32)).astype(jnp.int32)
    return jnp.stack([ordering // V, ordering % V]).astype(jnp.int32)


def draw_block_starts(key, part):
    blocks = pair_blocks(virt_labels(key))
    block_sizes = jnp.sum((blocks[:, None] == jnp.arange(8, dtype=jnp.int32)[None, :]).astype(jnp.int32), axis=0)
    return jnp.concatenate([jnp.zeros((1,), jnp.int32), jnp.cumsum(block_sizes)[:7].astype(jnp.int32)])


def draw_col_pairs(key, part):
    labels = virt_labels(key)
    key = jax.random.fold_in(key, 5)
    return partner_pairs(key, labels, V, CB)


def draw_row_pairs(key, part):
    key = jax.random.fold_in(key, 7)
    fixed_part = jnp.arange(8, dtype=jnp.int32)
    random_part = jax.random.randint(jax.random.fold_in(key, 3), (O - 8,), 0, 8, dtype=jnp.int32)
    labels = jax.random.permutation(jax.random.fold_in(key, 4), jnp.concatenate([fixed_part, random_part]))
    return partner_pairs(key, labels, O, RB)


def level_of(rng, shape, shards, least, largest):
    def one(position, blocks):
        heights = jax.random.uniform(jax.random.fold_in(jax.random.fold_in(rng, 6), position), (blocks,), jnp.float32, least / len(shards), largest / len(shards))
        return jnp.repeat(jnp.exp(heights), shape[position] // blocks).reshape((-1,) + (1,) * (len(shape) - position - 1))

    level = one(*shards[0])
    for cut in shards[1:]:
        level = level * one(*cut)
    return level


def gaussian(rng, extent, width, limit, cuts=(), held_as=jnp.bfloat16):
    loudness = level_of(rng, extent, cuts, -0.22, 0.18) if cuts else 1.0
    result = jax.random.normal(rng, extent, jnp.float32) * width * loudness
    return jnp.minimum(jnp.maximum(result, -limit), limit).astype(held_as)


def setup_inputs(seed: int = 0) -> dict:
    key_of = jax.random.split(jax.random.key(seed), 13)
    return {
        "t2_packed": gaussian(key_of[0], (RB, NCD), 1.0, 6.0, ((1, 256),), jnp.float32),
        "w_packed": gaussian(key_of[1], (NCD, CB), (V * V // 8) ** -0.5, 0.015625, ((0, 256),), jnp.float32),
        "pair_list": draw_pair_list(jax.random.fold_in(key_of[12], 71), 0),
        "block_starts": draw_block_starts(jax.random.fold_in(key_of[12], 71), 0),
        "singles": gaussian(key_of[4], (O, V), 0.5, 3.0, (), jnp.float32),
        "row_pairs": draw_row_pairs(jax.random.fold_in(key_of[12], 71), 0),
        "col_pairs": draw_col_pairs(jax.random.fold_in(key_of[12], 71), 0),
        "t2_slab": gaussian(key_of[7], (GROUPS, RB, CB), 1.0, 6.0, ((1, 64), (2, 4)), jnp.float32),
        "w_hole": gaussian(key_of[8], (GROUPS, RB, RB), RB ** -0.5, 0.375, ((1, 64),), jnp.float32),
        "driver": gaussian(key_of[9], (GROUPS, RB, CB), 1.0, 6.0, ((1, 64), (2, 4)), jnp.float32),
        "occ_energy": jnp.clip(jax.random.uniform(key_of[10], (O,), jnp.float32, -2.0, -0.5), -2.0, -0.5),
        "vir_energy": jnp.clip(jax.random.uniform(key_of[11], (V,), jnp.float32, 0.2, 3.0), 0.2, 3.0),
    }


def block_of(positions, block_starts):
    return jnp.sum((positions[:, None] >= block_starts[None, 1:]).astype(jnp.int32), axis=1)


def pair_terms(singles, row_pairs, group, orbit_c, orbit_d):
    left_rows = jnp.take(singles, row_pairs[group, :, 0], axis=0)
    right_rows = jnp.take(singles, row_pairs[group, :, 1], axis=0)
    return jnp.take(left_rows, orbit_c, axis=1) * jnp.take(right_rows, orbit_d, axis=1)


def ladder_pieces(t2_piece, w_piece, pair_piece, positions, block_starts, singles, row_pairs):
    blocks = block_of(positions, block_starts)
    first_block = blocks[0]
    final_block = blocks[blocks.shape[0] - 1]
    in_first = (blocks == first_block)[None, :]
    first_terms = pair_terms(singles, row_pairs, first_block, pair_piece[0], pair_piece[1])
    final_terms = pair_terms(singles, row_pairs, final_block, pair_piece[0], pair_piece[1])
    dressed = t2_piece + jnp.where(in_first, first_terms, final_terms)
    empty_like = jnp.zeros_like(dressed)
    first_part = jnp.dot(jnp.where(in_first, dressed, empty_like), w_piece, precision=lax.Precision.HIGHEST, preferred_element_type=jnp.float32)
    second_part = jnp.dot(jnp.where(in_first, empty_like, dressed), w_piece, precision=lax.Precision.HIGHEST, preferred_element_type=jnp.float32)
    return first_block, final_block, first_part, second_part


def slab_dressing(t2_slab, singles, rows, cols):
    left_rows = jnp.take(singles, rows[:, :, 0], axis=0)
    right_rows = jnp.take(singles, rows[:, :, 1], axis=0)
    target = (rows.shape[0], rows.shape[1], cols.shape[1])
    index_a = jnp.broadcast_to(cols[:, None, :, 0], target)
    index_b = jnp.broadcast_to(cols[:, None, :, 1], target)
    return t2_slab + jnp.take_along_axis(left_rows, index_a, axis=2) * jnp.take_along_axis(right_rows, index_b, axis=2)


def denominators(rows, cols, occ_energy, vir_energy):
    virtual_sum = vir_energy[cols[:, None, :, 0]] + vir_energy[cols[:, None, :, 1]]
    return virtual_sum - occ_energy[rows[:, :, None, 0]] - occ_energy[rows[:, :, None, 1]]


def reference(t2_packed, w_packed, pair_list, block_starts, singles, row_pairs, col_pairs, t2_slab, w_hole, driver, occ_energy, vir_energy):
    pieces = N_VIRT * N_REP
    columns = NCD // pieces

    def add_piece(piece, running):
        offset = (jnp.asarray(piece) * columns).astype(jnp.int32)
        positions = offset + jnp.arange(columns, dtype=jnp.int32)
        t2_piece = lax.dynamic_slice_in_dim(t2_packed, offset, columns, 1)
        w_piece = lax.dynamic_slice_in_dim(w_packed, offset, columns, 0)
        pair_piece = lax.dynamic_slice_in_dim(pair_list, offset, columns, 1)
        first_block, final_block, first_part, second_part = ladder_pieces(t2_piece, w_piece, pair_piece, positions, block_starts, singles, row_pairs)
        return running.at[first_block].add(first_part).at[final_block].add(second_part)

    ladder = lax.fori_loop(0, pieces, add_piece, jnp.zeros((GROUPS, RB, CB), jnp.float32))
    slab_dressed = slab_dressing(t2_slab, singles, row_pairs, col_pairs)
    hole_term = jnp.einsum("hrk,hkq->hrq", w_hole, slab_dressed, precision=lax.Precision.HIGHEST)
    denominator = denominators(row_pairs, col_pairs, occ_energy, vir_energy)
    return (driver + ladder + hole_term) / denominator
```

```python
import jax
import jax.numpy as jnp
from jax import lax
from jax.experimental import pallas as pl
from jax.experimental.pallas import tpu as pltpu
from jax.sharding import PartitionSpec as P

MESH = pl.DeviceIdType.MESH
F32 = jnp.float32
BF16 = jnp.bfloat16
I32 = jnp.int32

GROUPS = 8
OCC = 120
VIRT = 960
ROWS = 256
COLS = 512
PIECE = 3600
STEP = 720
STEPS = PIECE // STEP
NZ = 8
NY = 4
NX = 4
PLACES = NZ * NY
PLACE = 8 * PIECE
HALF = PLACES // 2


def split(value):
    high = value.astype(BF16)
    return high, (value - high.astype(F32)).astype(BF16)


def block_at(starts, position):
    block = jnp.int32(0)
    for h in range(1, GROUPS):
        block += (position >= starts[h]).astype(I32)
    return block


def over_rows(left, right):
    return lax.dot_general(left, right, (((0,), (0,)), ((), ())), preferred_element_type=F32)


def ladder_kernel(
    starts, singles, pairs, rows, t2_hbm, w_hbm, out_a, out_b, t2, w, pair, padded, table, select, sems
):
    copies = []
    for k in range(STEPS):
        copies.append(
            (
                pltpu.make_async_copy(t2_hbm.at[k], t2.at[k], sems.at[0, k]),
                pltpu.make_async_copy(w_hbm.at[k], w.at[k], sems.at[1, k]),
            )
        )
        for copy in copies[-1]:
            copy.start()
    segment = lax.axis_index("virt") * NX + lax.axis_index("rep")
    place = lax.axis_index("virt") // 2
    block_a = block_at(starts, place * PLACE)
    block_b = block_at(starts, place * PLACE + PLACE - 1)
    count = jnp.clip(starts[block_b] - segment * PIECE, 0, PIECE)
    mixed = jnp.minimum(count // STEP, STEPS - 1)

    padded[...] = jnp.zeros_like(padded)
    padded[0:OCC, 0:VIRT] = singles[...]
    high, low = split(padded[...].T)
    table[:, 0:128] = high
    table[:, 128:256] = low
    for k in range(STEPS):
        part = pairs[:, k * STEP : (k + 1) * STEP]
        pair[k] = jnp.concatenate([part, jnp.zeros((6, STEP), I32)], axis=0).T
    orbit = lax.broadcasted_iota(I32, (128, ROWS), 0)
    for s, block in enumerate((block_a, block_b)):
        for side in range(2):
            hit = (orbit == rows[block, side : side + 1, :]).astype(F32)
            select[s, side] = jnp.concatenate([hit, hit], axis=0).astype(BF16)
    out_a[...] = jnp.zeros_like(out_a)
    out_b[...] = jnp.zeros_like(out_b)

    def gathered(k, side):
        index = pair[k][:, side : side + 1]
        hit = (lax.broadcasted_iota(I32, (STEP, 1024), 1) == index).astype(BF16)
        return jnp.dot(hit, table[...], preferred_element_type=F32).astype(BF16)

    def dressed(k, orbit_c, orbit_d, select_i, select_j):
        left = jnp.dot(orbit_c, select_i, preferred_element_type=F32)
        right = jnp.dot(orbit_d, select_j, preferred_element_type=F32)
        return t2[k] + left * right

    def product(value, k):
        value_high, value_low = split(value)
        w_high, w_low = split(w[k])
        return (
            over_rows(value_high, w_high) + over_rows(value_high, w_low) + over_rows(value_low, w_high)
        )

    def step(k, carry):
        pltpu.make_async_copy(t2_hbm.at[k], t2.at[k], sems.at[0, k]).wait()
        pltpu.make_async_copy(w_hbm.at[k], w.at[k], sems.at[1, k]).wait()
        in_a = k < mixed
        value = dressed(
            k,
            gathered(k, 0),
            gathered(k, 1),
            jnp.where(in_a, select[0, 0], select[1, 0]),
            jnp.where(in_a, select[0, 1], select[1, 1]),
        )
        part = product(value, k)
        out_a[...] += part * jnp.where(k < mixed, 1.0, 0.0)
        out_b[...] += part * jnp.where(k > mixed, 1.0, 0.0)
        return carry

    lax.fori_loop(0, STEPS, step, 0)
    orbit_c = gathered(mixed, 0)
    orbit_d = gathered(mixed, 1)
    mask = lax.broadcasted_iota(I32, (STEP, ROWS), 0) < count - mixed * STEP
    value_a = jnp.where(mask, dressed(mixed, orbit_c, orbit_d, select[0, 0], select[0, 1]), 0.0)
    out_a[...] += product(value_a, mixed)
    value_b = jnp.where(mask, 0.0, dressed(mixed, orbit_c, orbit_d, select[1, 0], select[1, 1]))
    out_b[...] += product(value_b, mixed)


def lookup(columns, index):
    low = index & 127
    tile = index >> 7
    found = jnp.zeros((8, 128), F32)
    for t in range(8):
        piece = jnp.take_along_axis(
            columns[:, 128 * t : 128 * (t + 1)], low, axis=1, mode="promise_in_bounds"
        )
        found = jnp.where(tile == t, piece, found)
    return found


def exchange_kernel(
    starts,
    part_a,
    part_b,
    singles,
    rows,
    cols,
    t2_slab,
    w_hole,
    driver,
    occ,
    vir,
    out,
    mine,
    give,
    got,
    ring1,
    ring2,
    recv,
    slab_send,
    slab_recv,
    slab_all,
    hole_send,
    hole_recv,
    core_sems,
    ring_sems,
    all_sems,
    h1_sems,
    h2_sems,
    h3_sems,
):
    virt = lax.axis_index("virt")
    x = lax.axis_index("rep")
    core = lax.rem(virt, 2)
    place = virt // 2
    y = lax.rem(place, NY)
    z = place // NY
    xp = lax.rem(x + 1, NX)
    xo = lax.rem(x + 2, NX)
    xm = lax.rem(x + 3, NX)

    def device(place_to, core_to):
        return (place_to * 2 + core_to, x)

    barrier = pltpu.get_barrier_semaphore()

    def greet(target):
        pl.semaphore_signal(barrier, inc=1, device_id=target, device_id_type=MESH)

    greet(device(place, 1 - core))
    greet((virt, xp))
    greet((virt, xm))

    def greet_place(d, carry):
        greet(device(lax.rem(place + d, PLACES), core))
        return carry

    lax.fori_loop(1, PLACES, greet_place, 0)
    for d in range(1, NY):
        greet(device(z * NY + lax.rem(y + d, NY), 1 - core))

    upper = lax.broadcasted_iota(I32, (PLACES, 8, 128), 1) < 4
    for q in range(NX):
        a = part_a[:, 128 * q : 128 * (q + 1)].reshape(PLACES, 8, 128)
        b = part_b[:, 128 * q : 128 * (q + 1)].reshape(PLACES, 8, 128)
        tile0 = jnp.where(upper, a, pltpu.roll(b, 4, 1))
        tile1 = jnp.where(upper, pltpu.roll(a, 4, 1), b)
        mine[q] = jnp.where(core == 0, tile0, tile1)
        give[q] = jnp.where(core == 0, tile1, tile0)

    pl.semaphore_wait(barrier, 2 + PLACES - 1 + 1 + NY - 1)

    def core_copy(q):
        return pltpu.make_async_remote_copy(
            src_ref=give.at[q],
            dst_ref=got.at[q],
            send_sem=core_sems.at[0, q],
            recv_sem=core_sems.at[1, q],
            device_id=device(place, 1 - core),
            device_id_type=MESH,
        )

    for q in (xo, xp, xm, x):
        core_copy(q).start()

    row_index = []
    lane = lax.broadcasted_iota(I32, (GROUPS, ROWS), 1)
    for side in range(2):
        table = rows[:, side, :].astype(F32)
        for kk in range(4):
            hit = jnp.where(lane == virt * 4 + kk, table, 0.0)
            row_index.append(jnp.sum(hit, axis=1, keepdims=True).astype(I32))
    orbit = lax.broadcasted_iota(I32, (GROUPS, OCC), 1)
    hits = jnp.concatenate([(orbit == index).astype(F32) for index in row_index], axis=0)
    chosen = jnp.dot(hits, singles[...], precision=lax.Precision.HIGHEST, preferred_element_type=F32)
    chosen = jnp.concatenate([chosen, jnp.zeros((64, 64), F32)], axis=1)
    index_a = cols[:, 0, :]
    index_b = cols[:, 1, :]
    for kk in range(4):
        left = lookup(chosen[8 * kk : 8 * kk + 8], index_a)
        right = lookup(chosen[32 + 8 * kk : 40 + 8 * kk], index_b)
        value = t2_slab[:, kk, :] + left * right
        slab_send[:, kk, 0:128] = jnp.where(core == 0, value, 0.0)
        slab_send[:, 4 + kk, 0:128] = jnp.where(core == 0, 0.0, value)
        value = w_hole[:, kk, :]
        slab_send[:, kk, 128:384] = jnp.where(core == 0, value, 0.0)
        slab_send[:, 4 + kk, 128:384] = jnp.where(core == 0, 0.0, value)

    def h1_copy(d):
        to = lax.rem(z + d, NZ)
        return pltpu.make_async_remote_copy(
            src_ref=slab_send.at[to],
            dst_ref=slab_recv.at[z],
            send_sem=h1_sems.at[0, d],
            recv_sem=h1_sems.at[1, d],
            device_id=device(to * NY + y, core),
            device_id_type=MESH,
        )

    for d in range(1, NZ):
        h1_copy(d).start()
    slab_recv[z] = slab_send[z]

    def summed(q):
        core_copy(q).wait()
        mine[q] += got[q]

    def ring1_copy(way):
        lo = HALF * way
        return pltpu.make_async_remote_copy(
            src_ref=mine.at[xo, pl.ds(lo, HALF)],
            dst_ref=ring1.at[way],
            send_sem=ring_sems.at[0, way],
            recv_sem=ring_sems.at[1, way],
            device_id=(virt, xp if way == 0 else xm),
            device_id_type=MESH,
        )

    def ring2_copy(way, half):
        to = xp if way == 0 else xm
        return pltpu.make_async_remote_copy(
            src_ref=mine.at[to, pl.ds(HALF * half, HALF)],
            dst_ref=ring2.at[way, pl.ds(HALF * half, HALF)],
            send_sem=ring_sems.at[0, 2 + 2 * way + half],
            recv_sem=ring_sems.at[1, 2 + 2 * way + half],
            device_id=(virt, to),
            device_id_type=MESH,
        )

    summed(xo)
    ring1_copy(0).start()
    ring1_copy(1).start()
    summed(xp)
    ring2_copy(0, 1).start()
    summed(xm)
    ring2_copy(1, 0).start()

    def h2_copy(d):
        other = lax.rem(y * 2 + core + d, 2 * NY)
        return pltpu.make_async_remote_copy(
            src_ref=slab_recv.at[:, :, pl.ds(0, 128)],
            dst_ref=slab_all.at[core, :, y],
            send_sem=h2_sems.at[0, d],
            recv_sem=h2_sems.at[1, d],
            device_id=(z * 2 * NY + other, x),
            device_id_type=MESH,
        )

    for d in range(1, NZ):
        h1_copy(d).wait_recv()
    for d in range(1, 2 * NY):
        h2_copy(d).start()
    slab_all[core, :, y] = slab_recv[:, :, 0:128]

    ring1_copy(0).wait_recv()
    mine[xp, 0:HALF] += ring1[0]
    ring2_copy(0, 0).start()
    ring1_copy(1).wait_recv()
    mine[xm, HALF:PLACES] += ring1[1]
    ring2_copy(1, 1).start()
    summed(x)

    for d in range(1, 2 * NY):
        h2_copy(d).wait_recv()
    slab = (slab_all[0] + slab_all[1]).reshape(ROWS, 128)
    weights = slab_recv[:, :, 128:384].reshape(8 * NZ, ROWS)
    hole = jnp.dot(weights, slab, precision=lax.Precision.HIGHEST, preferred_element_type=F32)
    hole_send[...] = hole.reshape(NZ, 8, 128)

    def h3_copy(d):
        to = lax.rem(z + d, NZ)
        return pltpu.make_async_remote_copy(
            src_ref=hole_send.at[to],
            dst_ref=hole_recv.at[z],
            send_sem=h3_sems.at[0, d],
            recv_sem=h3_sems.at[1, d],
            device_id=device(to * NY + y, core),
            device_id_type=MESH,
        )

    for d in range(1, NZ):
        h3_copy(d).start()
    hole_recv[z] = hole_send[z]

    for way in range(2):
        for half in range(2):
            ring2_copy(way, half).wait_recv()
    mine[x] += ring2[0] + ring2[1]

    def all_copy(d):
        to = lax.rem(place + d, PLACES)
        return pltpu.make_async_remote_copy(
            src_ref=mine.at[x, to],
            dst_ref=recv.at[place],
            send_sem=all_sems.at[0, d],
            recv_sem=all_sems.at[1, d],
            device_id=device(to, core),
            device_id_type=MESH,
        )

    def all_start(d, carry):
        all_copy(d).start()
        return carry

    lax.fori_loop(1, PLACES, all_start, 0)
    recv[place] = mine[x, place]

    zeros = jnp.zeros((8, 64), F32)
    energy = jnp.concatenate([jnp.broadcast_to(vir[...], (8, VIRT)), zeros], axis=1)
    vir_sum = lookup(energy, index_a) + lookup(energy, index_b)
    occ_value = jnp.sum(hits * occ[...], axis=1, keepdims=True)
    column = lax.broadcasted_iota(I32, (32, PLACES * 8), 1)
    row = lax.broadcasted_iota(I32, (32, PLACES * 8), 0)
    position = (column >> 3) * PLACE + ((column >> 2) & 1) * (PLACE - 1)
    block = jnp.zeros_like(column)
    for h in range(1, GROUPS):
        block += (position >= starts[h]).astype(I32)
    pick = ((row & 7) == block) & ((row >> 3) == (column & 3))
    pick = pick.astype(F32)

    for d in range(1, NZ):
        h3_copy(d).wait_recv()

    def all_wait(d, carry):
        all_copy(d).wait()
        return carry

    lax.fori_loop(1, PLACES, all_wait, 0)
    ladder = jnp.dot(
        pick,
        recv[...].reshape(PLACES * 8, 128),
        precision=lax.Precision.HIGHEST,
        preferred_element_type=F32,
    )
    for kk in range(4):
        total = driver[:, kk, :] + ladder[8 * kk : 8 * kk + 8]
        total += hole_recv[:, kk, :] + hole_recv[:, 4 + kk, :]
        below = vir_sum - occ_value[8 * kk : 8 * kk + 8] - occ_value[32 + 8 * kk : 40 + 8 * kk]
        out[:, kk, :] = total / below

    for d in range(1, NZ):
        h1_copy(d).wait_send()
        h3_copy(d).wait_send()
        h2_copy(d).wait_send()
    for way in range(2):
        ring1_copy(way).wait_send()
        for half in range(2):
            ring2_copy(way, half).wait_send()


def body(
    t2_packed,
    w_packed,
    pair_list,
    block_starts,
    singles,
    row_pairs,
    col_pairs,
    t2_slab,
    w_hole,
    driver,
    occ_energy,
    vir_energy,
):
    vmem = pl.BlockSpec(memory_space=pltpu.VMEM)
    smem = pl.BlockSpec(memory_space=pltpu.SMEM)
    hbm = pl.BlockSpec(memory_space=pl.ANY)
    rows = row_pairs.transpose(0, 2, 1)
    cols = col_pairs.transpose(0, 2, 1)
    t2_steps = t2_packed.T.reshape(STEPS, STEP, ROWS)
    w_steps = w_packed.reshape(STEPS, STEP, COLS)
    part_a, part_b = pl.pallas_call(
        ladder_kernel,
        out_shape=[jax.ShapeDtypeStruct((ROWS, COLS), F32)] * 2,
        in_specs=[smem, vmem, vmem, vmem, hbm, hbm],
        out_specs=[vmem, vmem],
        scratch_shapes=[
            pltpu.VMEM((STEPS, STEP, ROWS), F32),
            pltpu.VMEM((STEPS, STEP, COLS), F32),
            pltpu.VMEM((STEPS, STEP, 8), I32),
            pltpu.VMEM((128, 1024), F32),
            pltpu.VMEM((1024, 256), BF16),
            pltpu.VMEM((2, 2, 256, ROWS), BF16),
            pltpu.SemaphoreType.DMA((2, STEPS)),
        ],
        compiler_params=pltpu.CompilerParams(vmem_limit_bytes=50 * 2**20),
        name="ladder",
    )(block_starts, singles, pair_list, rows, t2_steps, w_steps)
    tiles = (NX, PLACES, 8, 128)
    return pl.pallas_call(
        exchange_kernel,
        out_shape=jax.ShapeDtypeStruct((GROUPS, 4, 128), F32),
        in_specs=[smem] + [vmem] * 10,
        out_specs=vmem,
        scratch_shapes=[
            pltpu.VMEM(tiles, F32),
            pltpu.VMEM(tiles, F32),
            pltpu.VMEM(tiles, F32),
            pltpu.VMEM((2, HALF, 8, 128), F32),
            pltpu.VMEM((2, PLACES, 8, 128), F32),
            pltpu.VMEM((PLACES, 8, 128), F32),
            pltpu.VMEM((NZ, 8, 384), F32),
            pltpu.VMEM((NZ, 8, 384), F32),
            pltpu.VMEM((2, NZ, NY, 8, 128), F32),
            pltpu.VMEM((NZ, 8, 128), F32),
            pltpu.VMEM((NZ, 8, 128), F32),
            pltpu.SemaphoreType.DMA((2, NX)),
            pltpu.SemaphoreType.DMA((2, 6)),
            pltpu.SemaphoreType.DMA((2, PLACES)),
            pltpu.SemaphoreType.DMA((2, NZ)),
            pltpu.SemaphoreType.DMA((2, 2 * NY)),
            pltpu.SemaphoreType.DMA((2, NZ)),
        ],
        compiler_params=pltpu.CompilerParams(
            collective_id=0, has_side_effects=True, vmem_limit_bytes=40 * 2**20
        ),
        name="exchange",
    )(
        block_starts,
        part_a,
        part_b,
        singles,
        rows,
        cols,
        t2_slab,
        w_hole,
        driver,
        occ_energy.reshape(1, OCC),
        vir_energy.reshape(1, VIRT),
    )


def solution(mesh):
    in_specs = (
        P(None, ("virt", "rep")),
        P(("virt", "rep"), None),
        P(None, ("virt", "rep")),
        P(),
        P(),
        P(),
        P(None, "rep", None),
        P(None, "virt", "rep"),
        P(None, "virt", None),
        P(None, "virt", "rep"),
        P(),
        P(),
    )
    out_specs = P(None, "virt", "rep")
    return jax.shard_map(body, mesh=mesh, in_specs=in_specs, out_specs=out_specs, check_vma=False)
```

```python
import jax
import jax.numpy as jnp
from jax import lax
from jax.experimental import pallas as pl
from jax.experimental.pallas import tpu as pltpu
from jax.sharding import PartitionSpec as P

MESH = pl.DeviceIdType.MESH
F32 = jnp.float32
BF16 = jnp.bfloat16
I32 = jnp.int32

GROUPS = 8
OCC = 120
VIRT = 960
ROWS = 256
COLS = 512
PIECE = 3600
STEP = 240
STEPS = PIECE // STEP
JOIN = 3
CHUNK = STEP * JOIN
CHUNKS = STEPS // JOIN
NZ = 8
NY = 4
NX = 4
PLACES = NZ * NY
PLACE = 8 * PIECE
PARTS = 4
PART = PLACES // PARTS
HALF = PART // 2


def split(value):
    high = value.astype(BF16)
    return high, (value - high.astype(F32)).astype(BF16)


def block_at(starts, position):
    block = jnp.int32(0)
    for h in range(1, GROUPS):
        block += (position >= starts[h]).astype(I32)
    return block


def over_rows(left, right):
    return lax.dot_general(left, right, (((0,), (0,)), ((), ())), preferred_element_type=F32)


def lookup(columns, index):
    low = index & 127
    tile = index >> 7
    found = jnp.zeros((8, 128), F32)
    for t in range(8):
        piece = jnp.take_along_axis(
            columns[:, 128 * t : 128 * (t + 1)], low, axis=1, mode="promise_in_bounds"
        )
        found = jnp.where(tile == t, piece, found)
    return found


def ladder_kernel(
    starts_hbm,
    singles_hbm,
    pairs_hbm,
    rows_hbm,
    cols_hbm,
    slab_hbm,
    hole_hbm,
    driver_hbm,
    occ_hbm,
    vir_hbm,
    t2_hbm,
    w_hbm,
    out,
    starts,
    singles,
    pairs,
    rows,
    cols,
    t2_slab,
    w_hole,
    driver,
    occ,
    vir,
    t2,
    w,
    pair,
    padded,
    table,
    select,
    sum_a,
    sum_b,
    mine,
    give,
    got,
    ring1,
    ring2,
    recv,
    slab_send,
    slab_recv,
    slab_all,
    hole_send,
    hole_recv,
    small_sems,
    load_sems,
    core_sems,
    ring_sems,
    all_sems,
    h1_sems,
    h2_sems,
    h3_sems,
):
    virt = lax.axis_index("virt")
    x = lax.axis_index("rep")
    core = lax.rem(virt, 2)
    place = virt // 2
    y = lax.rem(place, NY)
    z = place // NY
    xp = lax.rem(x + 1, NX)
    xo = lax.rem(x + 2, NX)
    xm = lax.rem(x + 3, NX)

    small = [
        pltpu.make_async_copy(source, target, small_sems.at[n])
        for n, (source, target) in enumerate(
            (
                (starts_hbm, starts),
                (singles_hbm, singles),
                (pairs_hbm, pairs),
                (rows_hbm, rows),
                (cols_hbm, cols),
                (slab_hbm, t2_slab),
                (hole_hbm, w_hole),
                (driver_hbm, driver),
                (occ_hbm, occ),
                (vir_hbm, vir),
            )
        )
    ]
    for copy in small:
        copy.start()

    def load(k):
        piece = pl.ds(k * JOIN, JOIN)
        return (
            pltpu.make_async_copy(t2_hbm.at[piece], t2.at[piece], load_sems.at[0, k]),
            pltpu.make_async_copy(w_hbm.at[piece], w.at[piece], load_sems.at[1, k]),
        )

    for k in range(CHUNKS):
        for copy in load(k):
            copy.start()

    def device(place_to, core_to):
        return (place_to * 2 + core_to, x)

    barrier = pltpu.get_barrier_semaphore()

    def greet(target):
        pl.semaphore_signal(barrier, inc=1, device_id=target, device_id_type=MESH)

    greet(device(place, 1 - core))
    greet((virt, xp))
    greet((virt, xm))

    def greet_place(d, carry):
        greet(device(lax.rem(place + d, PLACES), core))
        return carry

    lax.fori_loop(1, PLACES, greet_place, 0)
    for d in range(1, NY):
        greet(device(z * NY + lax.rem(y + d, NY), 1 - core))

    for copy in small:
        copy.wait()

    segment = virt * NX + x
    block_a = block_at(starts, place * PLACE)
    block_b = block_at(starts, place * PLACE + PLACE - 1)
    count = jnp.clip(starts[block_b] - segment * PIECE, 0, PIECE)
    mixed = jnp.minimum(count // STEP, STEPS - 1)
    padded[...] = jnp.zeros_like(padded)
    padded[0:OCC, 0:VIRT] = singles[...]
    high, low = split(padded[...].T)
    table[:, 0:128] = high
    table[:, 128:256] = low
    for k in range(STEPS):
        part = pairs[:, k * STEP : (k + 1) * STEP]
        pair[k] = jnp.concatenate([part, jnp.zeros((6, STEP), I32)], axis=0).T
    orbit = lax.broadcasted_iota(I32, (128, ROWS), 0)
    for s, block in enumerate((block_a, block_b)):
        for side in range(2):
            hit = (orbit == rows[block, side : side + 1, :]).astype(F32)
            select[s, side] = jnp.concatenate([hit, hit], axis=0).astype(BF16)
    sum_a[...] = jnp.zeros_like(sum_a)
    sum_b[...] = jnp.zeros_like(sum_b)

    row_index = []
    lane = lax.broadcasted_iota(I32, (GROUPS, ROWS), 1)
    for side in range(2):
        both = rows[:, side, :].astype(F32)
        for kk in range(4):
            hit = jnp.where(lane == virt * 4 + kk, both, 0.0)
            row_index.append(jnp.sum(hit, axis=1, keepdims=True).astype(I32))
    orbit = lax.broadcasted_iota(I32, (GROUPS, OCC), 1)
    hits = jnp.concatenate([(orbit == index).astype(F32) for index in row_index], axis=0)
    chosen = jnp.dot(hits, singles[...], precision=lax.Precision.HIGHEST, preferred_element_type=F32)
    chosen = jnp.concatenate([chosen, jnp.zeros((64, 64), F32)], axis=1)
    index_a = cols[:, 0, :]
    index_b = cols[:, 1, :]
    for kk in range(4):
        left = lookup(chosen[8 * kk : 8 * kk + 8], index_a)
        right = lookup(chosen[32 + 8 * kk : 40 + 8 * kk], index_b)
        value = t2_slab[:, kk, :] + left * right
        slab_send[:, kk, 0:128] = jnp.where(core == 0, value, 0.0)
        slab_send[:, 4 + kk, 0:128] = jnp.where(core == 0, 0.0, value)
        value = w_hole[:, kk, :]
        slab_send[:, kk, 128:384] = jnp.where(core == 0, value, 0.0)
        slab_send[:, 4 + kk, 128:384] = jnp.where(core == 0, 0.0, value)

    def gathered(index):
        hit = (lax.broadcasted_iota(I32, (index.shape[0], 1024), 1) == index).astype(BF16)
        return jnp.dot(hit, table[...], preferred_element_type=F32).astype(BF16)

    def dressed(k, orbit_c, orbit_d, select_i, select_j):
        left = jnp.dot(orbit_c, select_i, preferred_element_type=F32)
        right = jnp.dot(orbit_d, select_j, preferred_element_type=F32)
        return t2[k] + left * right

    def product(value, k):
        value_high, value_low = split(value)
        w_high, w_low = split(w[k])
        return (
            over_rows(value_high, w_high) + over_rows(value_high, w_low) + over_rows(value_low, w_high)
        )

    def chunk(k):
        for copy in load(k):
            copy.wait()
        index = pair[pl.ds(k * JOIN, JOIN)].reshape(CHUNK, 8)
        orbit_c = gathered(index[:, 0:1])
        orbit_d = gathered(index[:, 1:2])
        for s in range(JOIN):
            step = k * JOIN + s
            piece = slice(s * STEP, (s + 1) * STEP)
            in_a = step < mixed
            value = dressed(
                step,
                orbit_c[piece],
                orbit_d[piece],
                jnp.where(in_a, select[0, 0], select[1, 0]),
                jnp.where(in_a, select[0, 1], select[1, 1]),
            )
            part = product(value, step)
            sum_a[...] += part * jnp.where(step < mixed, 1.0, 0.0)
            sum_b[...] += part * jnp.where(step > mixed, 1.0, 0.0)

    def h1_copy(d):
        to = lax.rem(z + d, NZ)
        return pltpu.make_async_remote_copy(
            src_ref=slab_send.at[to],
            dst_ref=slab_recv.at[z],
            send_sem=h1_sems.at[0, d],
            recv_sem=h1_sems.at[1, d],
            device_id=device(to * NY + y, core),
            device_id_type=MESH,
        )

    def h2_copy(d):
        other = lax.rem(y * 2 + core + d, 2 * NY)
        return pltpu.make_async_remote_copy(
            src_ref=slab_recv.at[:, :, pl.ds(0, 128)],
            dst_ref=slab_all.at[core, :, y],
            send_sem=h2_sems.at[0, d],
            recv_sem=h2_sems.at[1, d],
            device_id=(z * 2 * NY + other, x),
            device_id_type=MESH,
        )

    def h3_copy(d):
        to = lax.rem(z + d, NZ)
        return pltpu.make_async_remote_copy(
            src_ref=hole_send.at[to],
            dst_ref=hole_recv.at[z],
            send_sem=h3_sems.at[0, d],
            recv_sem=h3_sems.at[1, d],
            device_id=device(to * NY + y, core),
            device_id_type=MESH,
        )

    chunk(0)
    pl.semaphore_wait(barrier, 2 + PLACES - 1 + 1 + NY - 1)
    for d in range(1, NZ):
        h1_copy(d).start()
    slab_recv[z] = slab_send[z]
    chunk(1)
    for d in range(1, NZ):
        h1_copy(d).wait_recv()
    for d in range(1, 2 * NY):
        h2_copy(d).start()
    slab_all[core, :, y] = slab_recv[:, :, 0:128]
    chunk(2)
    chunk(3)
    for d in range(1, 2 * NY):
        h2_copy(d).wait_recv()
    slab = (slab_all[0] + slab_all[1]).reshape(ROWS, 128)
    weights = slab_recv[:, :, 128:384].reshape(8 * NZ, ROWS)
    hole = jnp.dot(weights, slab, precision=lax.Precision.HIGHEST, preferred_element_type=F32)
    hole_send[...] = hole.reshape(NZ, 8, 128)
    for d in range(1, NZ):
        h3_copy(d).start()
    hole_recv[z] = hole_send[z]
    chunk(4)

    index = pair[mixed]
    orbit_c = gathered(index[:, 0:1])
    orbit_d = gathered(index[:, 1:2])
    mask = lax.broadcasted_iota(I32, (STEP, ROWS), 0) < count - mixed * STEP
    value_a = jnp.where(mask, dressed(mixed, orbit_c, orbit_d, select[0, 0], select[0, 1]), 0.0)
    sum_a[...] += product(value_a, mixed)
    value_b = jnp.where(mask, 0.0, dressed(mixed, orbit_c, orbit_d, select[1, 0], select[1, 1]))
    sum_b[...] += product(value_b, mixed)

    def first(g):
        return lax.rem(z // 2 + 1 + g, PARTS) * PART

    def core_copy(g):
        tiles = pl.ds(first(g), PART)
        return pltpu.make_async_remote_copy(
            src_ref=give.at[:, tiles],
            dst_ref=got.at[:, tiles],
            send_sem=core_sems.at[0, g],
            recv_sem=core_sems.at[1, g],
            device_id=device(place, 1 - core),
            device_id_type=MESH,
        )

    def ring1_copy(g, way):
        return pltpu.make_async_remote_copy(
            src_ref=mine.at[xo, pl.ds(first(g) + HALF * way, HALF)],
            dst_ref=ring1.at[way, g],
            send_sem=ring_sems.at[0, g, way],
            recv_sem=ring_sems.at[1, g, way],
            device_id=(virt, xp if way == 0 else xm),
            device_id_type=MESH,
        )

    def ring2_copy(g, way, half):
        to = xp if way == 0 else xm
        tiles = pl.ds(first(g) + HALF * half, HALF)
        return pltpu.make_async_remote_copy(
            src_ref=mine.at[to, tiles],
            dst_ref=ring2.at[way, tiles],
            send_sem=ring_sems.at[0, g, 2 + 2 * way + half],
            recv_sem=ring_sems.at[1, g, 2 + 2 * way + half],
            device_id=(virt, to),
            device_id_type=MESH,
        )

    def all_copy(d):
        to = lax.rem(place + d, PLACES)
        return pltpu.make_async_remote_copy(
            src_ref=mine.at[x, to],
            dst_ref=recv.at[place],
            send_sem=all_sems.at[0, d],
            recv_sem=all_sems.at[1, d],
            device_id=device(to, core),
            device_id_type=MESH,
        )

    upper = lax.broadcasted_iota(I32, (PART, 8, 128), 1) < 4
    for g in range(PARTS):
        rows_of = pl.ds(pl.multiple_of(first(g) * 8, 8 * PART), 8 * PART)
        tiles = pl.ds(first(g), PART)
        for q in range(NX):
            a = sum_a[rows_of, 128 * q : 128 * (q + 1)].reshape(PART, 8, 128)
            b = sum_b[rows_of, 128 * q : 128 * (q + 1)].reshape(PART, 8, 128)
            tile0 = jnp.where(upper, a, pltpu.roll(b, 4, 1))
            tile1 = jnp.where(upper, pltpu.roll(a, 4, 1), b)
            mine[q, tiles] = jnp.where(core == 0, tile0, tile1)
            give[q, tiles] = jnp.where(core == 0, tile1, tile0)
        core_copy(g).start()

    zeros = jnp.zeros((8, 64), F32)
    energy = jnp.concatenate([jnp.broadcast_to(vir[...], (8, VIRT)), zeros], axis=1)
    vir_sum = lookup(energy, index_a) + lookup(energy, index_b)
    occ_value = jnp.sum(hits * occ[...], axis=1, keepdims=True)
    column = lax.broadcasted_iota(I32, (32, PLACES * 8), 1)
    row = lax.broadcasted_iota(I32, (32, PLACES * 8), 0)
    position = (column >> 3) * PLACE + ((column >> 2) & 1) * (PLACE - 1)
    block = jnp.zeros_like(column)
    for h in range(1, GROUPS):
        block += (position >= starts[h]).astype(I32)
    pick = ((row & 7) == block) & ((row >> 3) == (column & 3))
    pick = pick.astype(F32)

    for g in range(PARTS):
        tiles = pl.ds(first(g), PART)
        core_copy(g).wait()
        mine[:, tiles] += got[:, tiles]
        for way in range(2):
            ring1_copy(g, way).start()
        ring2_copy(g, 0, 1).start()
        ring2_copy(g, 1, 0).start()
    for g in range(PARTS):
        for way, to in ((0, xp), (1, xm)):
            tiles = pl.ds(first(g) + HALF * way, HALF)
            ring1_copy(g, way).wait_recv()
            mine[to, tiles] += ring1[way, g]
            ring2_copy(g, way, way).start()
    for g in range(PARTS):
        tiles = pl.ds(first(g), PART)
        for way in range(2):
            for half in range(2):
                ring2_copy(g, way, half).wait_recv()
        mine[x, tiles] += ring2[0, tiles] + ring2[1, tiles]

        def all_start(n, carry):
            d = lax.rem(first(g) + n - place + PLACES, PLACES)

            @pl.when(d > 0)
            def _():
                all_copy(d).start()

            return carry

        lax.fori_loop(0, PART, all_start, 0)
    recv[place] = mine[x, place]

    for d in range(1, NZ):
        h3_copy(d).wait_recv()

    def all_wait(d, carry):
        all_copy(d).wait()
        return carry

    lax.fori_loop(1, PLACES, all_wait, 0)
    ladder = jnp.dot(
        pick,
        recv[...].reshape(PLACES * 8, 128),
        precision=lax.Precision.HIGHEST,
        preferred_element_type=F32,
    )
    for kk in range(4):
        total = driver[:, kk, :] + ladder[8 * kk : 8 * kk + 8]
        total += hole_recv[:, kk, :] + hole_recv[:, 4 + kk, :]
        below = vir_sum - occ_value[8 * kk : 8 * kk + 8] - occ_value[32 + 8 * kk : 40 + 8 * kk]
        out[:, kk, :] = total / below

    for d in range(1, NZ):
        h1_copy(d).wait_send()
        h3_copy(d).wait_send()
        h2_copy(d).wait_send()
    for g in range(PARTS):
        for way in range(2):
            ring1_copy(g, way).wait_send()
            for half in range(2):
                ring2_copy(g, way, half).wait_send()


def body(
    t2_packed,
    w_packed,
    pair_list,
    block_starts,
    singles,
    row_pairs,
    col_pairs,
    t2_slab,
    w_hole,
    driver,
    occ_energy,
    vir_energy,
):
    hbm = pl.BlockSpec(memory_space=pl.ANY)
    tiles = (NX, PLACES, 8, 128)
    return pl.pallas_call(
        ladder_kernel,
        out_shape=jax.ShapeDtypeStruct((GROUPS, 4, 128), F32),
        in_specs=[hbm] * 12,
        out_specs=pl.BlockSpec(memory_space=pltpu.VMEM),
        scratch_shapes=[
            pltpu.SMEM((GROUPS,), I32),
            pltpu.VMEM((OCC, VIRT), F32),
            pltpu.VMEM((2, PIECE), I32),
            pltpu.VMEM((GROUPS, 2, ROWS), I32),
            pltpu.VMEM((GROUPS, 2, 128), I32),
            pltpu.VMEM((GROUPS, 4, 128), F32),
            pltpu.VMEM((GROUPS, 4, ROWS), F32),
            pltpu.VMEM((GROUPS, 4, 128), F32),
            pltpu.VMEM((1, OCC), F32),
            pltpu.VMEM((1, VIRT), F32),
            pltpu.VMEM((STEPS, STEP, ROWS), F32),
            pltpu.VMEM((STEPS, STEP, COLS), F32),
            pltpu.VMEM((STEPS, STEP, 8), I32),
            pltpu.VMEM((128, 1024), F32),
            pltpu.VMEM((1024, 256), BF16),
            pltpu.VMEM((2, 2, 256, ROWS), BF16),
            pltpu.VMEM((ROWS, COLS), F32),
            pltpu.VMEM((ROWS, COLS), F32),
            pltpu.VMEM(tiles, F32),
            pltpu.VMEM(tiles, F32),
            pltpu.VMEM(tiles, F32),
            pltpu.VMEM((2, PARTS, HALF, 8, 128), F32),
            pltpu.VMEM((2, PLACES, 8, 128), F32),
            pltpu.VMEM((PLACES, 8, 128), F32),
            pltpu.VMEM((NZ, 8, 384), F32),
            pltpu.VMEM((NZ, 8, 384), F32),
            pltpu.VMEM((2, NZ, NY, 8, 128), F32),
            pltpu.VMEM((NZ, 8, 128), F32),
            pltpu.VMEM((NZ, 8, 128), F32),
            pltpu.SemaphoreType.DMA((10,)),
            pltpu.SemaphoreType.DMA((2, CHUNKS)),
            pltpu.SemaphoreType.DMA((2, PARTS)),
            pltpu.SemaphoreType.DMA((2, PARTS, 6)),
            pltpu.SemaphoreType.DMA((2, PLACES)),
            pltpu.SemaphoreType.DMA((2, NZ)),
            pltpu.SemaphoreType.DMA((2, 2 * NY)),
            pltpu.SemaphoreType.DMA((2, NZ)),
        ],
        compiler_params=pltpu.CompilerParams(
            collective_id=0, has_side_effects=True, vmem_limit_bytes=60 * 2**20
        ),
        name="ladder",
    )(
        block_starts,
        singles,
        pair_list,
        row_pairs.transpose(0, 2, 1),
        col_pairs.transpose(0, 2, 1),
        t2_slab,
        w_hole,
        driver,
        occ_energy.reshape(1, OCC),
        vir_energy.reshape(1, VIRT),
        t2_packed.T.reshape(STEPS, STEP, ROWS),
        w_packed.reshape(STEPS, STEP, COLS),
    )


def solution(mesh):
    in_specs = (
        P(None, ("virt", "rep")),
        P(("virt", "rep"), None),
        P(None, ("virt", "rep")),
        P(),
        P(),
        P(),
        P(None, "rep", None),
        P(None, "virt", "rep"),
        P(None, "virt", None),
        P(None, "virt", "rep"),
        P(),
        P(),
    )
    out_specs = P(None, "virt", "rep")
    return jax.shard_map(body, mesh=mesh, in_specs=in_specs, out_specs=out_specs, check_vma=False)
```

```python
import jax
import jax.numpy as jnp
from jax import lax
from jax.experimental import pallas as pl
from jax.experimental.pallas import tpu as pltpu
from jax.sharding import PartitionSpec as P

MESH = pl.DeviceIdType.MESH
F32 = jnp.float32
BF16 = jnp.bfloat16
I32 = jnp.int32

GROUPS = 8
OCC = 120
VIRT = 960
ROWS = 256
COLS = 512
PIECE = 3600
CHUNK = 720
CHUNKS = PIECE // CHUNK
WIDE = COLS // 2
NZ = 8
NY = 4
NX = 4
PLACES = NZ * NY
PLACE = 8 * PIECE
PARTS = 4
PART = PLACES // PARTS
HALF = PLACES // 2


def split(value):
    high = value.astype(BF16)
    return high, (value - high.astype(F32)).astype(BF16)


def block_at(starts, position):
    block = jnp.int32(0)
    for h in range(1, GROUPS):
        block += (position >= starts[h]).astype(I32)
    return block


def over_rows(left, right):
    return lax.dot_general(left, right, (((0,), (0,)), ((), ())), preferred_element_type=F32)


def lookup(columns, index):
    low = index & 127
    tile = index >> 7
    found = jnp.zeros((8, 128), F32)
    for t in range(8):
        piece = jnp.take_along_axis(
            columns[:, 128 * t : 128 * (t + 1)], low, axis=1, mode="promise_in_bounds"
        )
        found = jnp.where(tile == t, piece, found)
    return found


def ladder_kernel(
    starts_hbm,
    singles_hbm,
    pairs_hbm,
    rows_hbm,
    cols_hbm,
    slab_hbm,
    hole_hbm,
    driver_hbm,
    occ_hbm,
    vir_hbm,
    t2_hbm,
    w_hbm,
    out,
    starts,
    singles,
    pairs,
    rows,
    cols,
    t2_slab,
    w_hole,
    driver,
    occ,
    vir,
    t2,
    w,
    pair,
    padded,
    table,
    select,
    sum_a,
    sum_b,
    mine,
    give,
    got,
    ring1,
    ring2,
    recv,
    orbits,
    d_high,
    d_low,
    slab_send,
    slab_recv,
    slab_all,
    hole_send,
    hole_recv,
    small_sems,
    load_sems,
    core_sems,
    ring_sems,
    late_sems,
    all_sems,
    hole_sems,
):
    virt = lax.axis_index("virt")
    x = lax.axis_index("rep")
    core = lax.rem(virt, 2)
    place = virt // 2
    y = lax.rem(place, NY)
    z = place // NY
    xp = lax.rem(x + 1, NX)
    xo = lax.rem(x + 2, NX)
    xm = lax.rem(x + 3, NX)

    small = [
        pltpu.make_async_copy(source, target, small_sems.at[n])
        for n, (source, target) in enumerate(
            (
                (starts_hbm, starts),
                (singles_hbm, singles),
                (pairs_hbm, pairs),
                (rows_hbm, rows),
                (cols_hbm, cols),
                (slab_hbm, t2_slab),
                (hole_hbm, w_hole),
                (driver_hbm, driver),
                (occ_hbm, occ),
                (vir_hbm, vir),
            )
        )
    ]
    for copy in small:
        copy.start()

    def load_t2(k):
        return pltpu.make_async_copy(t2_hbm.at[k], t2.at[k], load_sems.at[0, k])

    def load_w(k):
        return pltpu.make_async_copy(w_hbm.at[k], w.at[k], load_sems.at[1, k])

    load_t2(0).start()
    load_t2(1).start()

    def device(place_to, core_to):
        return (place_to * 2 + core_to, x)

    barrier = pltpu.get_barrier_semaphore()

    def greet(target):
        pl.semaphore_signal(barrier, inc=1, device_id=target, device_id_type=MESH)

    greet(device(place, 1 - core))
    greet((virt, xp))
    greet((virt, xm))

    for d in range(1, PLACES):
        greet(device(lax.rem(place + d, PLACES), core))
    for d in range(1, NY):
        greet(device(z * NY + lax.rem(y + d, NY), 1 - core))

    for copy in small:
        copy.wait()

    segment = virt * NX + x
    block_a = block_at(starts, place * PLACE)
    block_b = block_at(starts, place * PLACE + PLACE - 1)
    count = jnp.clip(starts[block_b] - segment * PIECE, 0, PIECE)
    mixed = jnp.minimum(count // CHUNK, CHUNKS - 1)
    padded[...] = jnp.zeros_like(padded)
    padded[0:OCC, 0:VIRT] = singles[...]
    high, low = split(padded[...].T)
    table[:, 0:128] = high
    table[:, 128:256] = low
    for k in range(CHUNKS):
        part = pairs[:, k * CHUNK : (k + 1) * CHUNK]
        pair[k] = jnp.concatenate([part, jnp.zeros((6, CHUNK), I32)], axis=0).T
    orbit = lax.broadcasted_iota(I32, (128, ROWS), 0)
    for s, block in enumerate((block_a, block_b)):
        for side in range(2):
            hit = (orbit == rows[block, side : side + 1, :]).astype(F32)
            select[s, side] = jnp.concatenate([hit, hit], axis=0).astype(BF16)

    row_index = []
    lane = lax.broadcasted_iota(I32, (GROUPS, ROWS), 1)
    for side in range(2):
        both = rows[:, side, :].astype(F32)
        for kk in range(4):
            hit = jnp.where(lane == virt * 4 + kk, both, 0.0)
            row_index.append(jnp.sum(hit, axis=1, keepdims=True).astype(I32))
    orbit = lax.broadcasted_iota(I32, (GROUPS, OCC), 1)
    hits = jnp.concatenate([(orbit == index).astype(F32) for index in row_index], axis=0)
    chosen = jnp.dot(hits, singles[...], precision=lax.Precision.HIGHEST, preferred_element_type=F32)
    chosen = jnp.concatenate([chosen, jnp.zeros((64, 64), F32)], axis=1)
    index_a = cols[:, 0, :]
    index_b = cols[:, 1, :]
    for kk in range(4):
        left = lookup(chosen[8 * kk : 8 * kk + 8], index_a)
        right = lookup(chosen[32 + 8 * kk : 40 + 8 * kk], index_b)
        value = t2_slab[:, kk, :] + left * right
        slab_send[:, kk, 0:128] = jnp.where(core == 0, value, 0.0)
        slab_send[:, 4 + kk, 0:128] = jnp.where(core == 0, 0.0, value)
        value = w_hole[:, kk, :]
        slab_send[:, kk, 128:384] = jnp.where(core == 0, value, 0.0)
        slab_send[:, 4 + kk, 128:384] = jnp.where(core == 0, 0.0, value)

    def gathered(index):
        hit = (lax.broadcasted_iota(I32, (index.shape[0], 1024), 1) == index).astype(BF16)
        return jnp.dot(hit, table[...], preferred_element_type=F32).astype(BF16)

    def dressed(k, select_i, select_j):
        left = jnp.dot(orbits[0, k], select_i, preferred_element_type=F32)
        right = jnp.dot(orbits[1, k], select_j, preferred_element_type=F32)
        return t2[k] + left * right

    in_chunk = lax.broadcasted_iota(I32, (CHUNK, ROWS), 0)

    def dress(k):
        if k + 2 < CHUNKS:
            load_t2(k + 2).start()
        load_w(k).start()
        load_t2(k).wait()
        index = pair[k]
        orbits[0, k] = gathered(index[:, 0:1])
        orbits[1, k] = gathered(index[:, 1:2])
        in_a = k <= mixed
        value = dressed(
            k,
            jnp.where(in_a, select[0, 0], select[1, 0]),
            jnp.where(in_a, select[0, 1], select[1, 1]),
        )
        bound = jnp.where(k > mixed, CHUNK, count - k * CHUNK)
        d_high[k], d_low[k] = split(jnp.where(in_chunk < bound, value, 0.0))

    def dress_rest():
        value = dressed(mixed, select[1, 0], select[1, 1])
        value = jnp.where(in_chunk < count - mixed * CHUNK, 0.0, value)
        d_high[CHUNKS], d_low[CHUNKS] = split(value)

    def product(k, n, half):
        columns = pl.ds(pl.multiple_of(half * WIDE, WIDE), WIDE)
        w_high, w_low = split(w[n, :, columns])
        return (
            over_rows(d_high[k], w_high) + over_rows(d_high[k], w_low) + over_rows(d_low[k], w_high)
        )

    def multiply(k, half):
        part = product(k, k, half)
        sum_a[...] += part * jnp.where(k <= mixed, 1.0, 0.0)
        sum_b[...] += part * jnp.where(k > mixed, 1.0, 0.0)

    def h1_copy(d):
        to = lax.rem(z + d, NZ)
        return pltpu.make_async_remote_copy(
            src_ref=slab_send.at[to],
            dst_ref=slab_recv.at[z],
            send_sem=hole_sems.at[0, 0],
            recv_sem=hole_sems.at[1, 0],
            device_id=device(to * NY + y, core),
            device_id_type=MESH,
        )

    def h2_copy(d):
        other = lax.rem(y * 2 + core + d, 2 * NY)
        return pltpu.make_async_remote_copy(
            src_ref=slab_recv.at[:, :, pl.ds(0, 128)],
            dst_ref=slab_all.at[core, :, y],
            send_sem=hole_sems.at[0, 1],
            recv_sem=hole_sems.at[1, 1],
            device_id=(z * 2 * NY + other, x),
            device_id_type=MESH,
        )

    def h3_copy(d):
        to = lax.rem(z + d, NZ)
        return pltpu.make_async_remote_copy(
            src_ref=hole_send.at[to],
            dst_ref=hole_recv.at[z],
            send_sem=hole_sems.at[0, 2],
            recv_sem=hole_sems.at[1, 2],
            device_id=device(to * NY + y, core),
            device_id_type=MESH,
        )

    def wait_bytes(ref, sem):
        pltpu.make_async_copy(ref, ref, sem).wait()

    def h1_wait(end):
        wait_bytes(slab_recv.at[pl.ds(0, NZ - 1)], hole_sems.at[end, 0])

    def h2_wait(end):
        wait_bytes(slab_all.at[:, pl.ds(0, NZ - 1)], hole_sems.at[end, 1])

    def h3_wait(end):
        wait_bytes(hole_recv.at[pl.ds(0, NZ - 1)], hole_sems.at[end, 2])

    own = x // 2
    far = 1 - own
    odd = lax.rem(x, 2)
    way_far = 1 - odd
    way_own = odd
    to_far = jnp.where(odd == 0, xm, xp)
    to_own = jnp.where(odd == 0, xp, xm)

    def first(g):
        return lax.rem(z // 2 + 1 + g, PARTS) * PART

    def core_copy(half, tiles, n):
        part = (pl.ds(2 * half, 2), tiles)
        return pltpu.make_async_remote_copy(
            src_ref=give.at[part],
            dst_ref=got.at[part],
            send_sem=core_sems.at[0, n],
            recv_sem=core_sems.at[1, n],
            device_id=device(place, 1 - core),
            device_id_type=MESH,
        )

    def ring1_copy(way):
        return pltpu.make_async_remote_copy(
            src_ref=mine.at[xo, pl.ds(HALF * way, HALF)],
            dst_ref=ring1.at[way],
            send_sem=ring_sems.at[0, 0],
            recv_sem=ring_sems.at[1, 1 + way],
            device_id=(virt, xp if way == 0 else xm),
            device_id_type=MESH,
        )

    def ring2_copy(way, to, tiles, recv_sem):
        return pltpu.make_async_remote_copy(
            src_ref=mine.at[to, tiles],
            dst_ref=ring2.at[way, tiles],
            send_sem=ring_sems.at[0, 0],
            recv_sem=recv_sem,
            device_id=(virt, to),
            device_id_type=MESH,
        )

    def all_copy(to):
        return pltpu.make_async_remote_copy(
            src_ref=mine.at[x, to],
            dst_ref=recv.at[place],
            send_sem=all_sems.at[0],
            recv_sem=all_sems.at[1],
            device_id=device(to, core),
            device_id_type=MESH,
        )

    upper = lax.broadcasted_iota(I32, (PART, 8, 128), 1) < 4

    def assemble(half, g):
        rows_of = pl.ds(pl.multiple_of(first(g) * 8, 8 * PART), 8 * PART)
        tiles = pl.ds(first(g), PART)
        for j in range(2):
            a = sum_a[rows_of, 128 * j : 128 * (j + 1)].reshape(PART, 8, 128)
            b = sum_b[rows_of, 128 * j : 128 * (j + 1)].reshape(PART, 8, 128)
            tile0 = jnp.where(upper, a, pltpu.roll(b, 4, 1))
            tile1 = jnp.where(upper, pltpu.roll(a, 4, 1), b)
            mine[2 * half + j, tiles] = jnp.where(core == 0, tile0, tile1)
            give[2 * half + j, tiles] = jnp.where(core == 0, tile1, tile0)

    everything = pl.ds(0, PLACES)

    for k in range(CHUNKS):
        dress(k)
    dress_rest()
    pl.semaphore_wait(barrier, 2 + PLACES - 1 + 1 + NY - 1)
    for d in range(1, NZ):
        h1_copy(d).start()
    slab_recv[z] = slab_send[z]

    sum_a[...] = jnp.zeros_like(sum_a)
    sum_b[...] = jnp.zeros_like(sum_b)
    for k in range(CHUNKS):
        load_w(k).wait()
        multiply(k, far)
    sum_b[...] += product(CHUNKS, mixed, far)
    for g in range(PARTS):
        assemble(far, g)
    core_copy(far, everything, 0).start()

    h1_wait(1)
    for d in range(1, 2 * NY):
        h2_copy(d).start()
    slab_all[core, :, y] = slab_recv[:, :, 0:128]

    sum_a[...] = jnp.zeros_like(sum_a)
    sum_b[...] = jnp.zeros_like(sum_b)
    multiply(0, own)
    multiply(1, own)
    core_copy(far, everything, 0).wait()
    for j in range(2):
        mine[2 * far + j] += got[2 * far + j]
    for way in range(2):
        ring1_copy(way).start()
    ring2_copy(way_far, to_far, pl.ds(HALF * (1 - way_far), HALF), ring_sems.at[1, 0]).start()
    multiply(2, own)
    multiply(3, own)
    multiply(4, own)
    sum_b[...] += product(CHUNKS, mixed, own)
    for g in range(PARTS):
        assemble(own, g)
        core_copy(own, pl.ds(first(g), PART), 1 + g).start()

    zeros = jnp.zeros((8, 64), F32)
    energy = jnp.concatenate([jnp.broadcast_to(vir[...], (8, VIRT)), zeros], axis=1)
    vir_sum = lookup(energy, index_a) + lookup(energy, index_b)
    occ_value = jnp.sum(hits * occ[...], axis=1, keepdims=True)
    column = lax.broadcasted_iota(I32, (32, PLACES * 8), 1)
    row = lax.broadcasted_iota(I32, (32, PLACES * 8), 0)
    position = (column >> 3) * PLACE + ((column >> 2) & 1) * (PLACE - 1)
    block = jnp.zeros_like(column)
    for h in range(1, GROUPS):
        block += (position >= starts[h]).astype(I32)
    pick = ((row & 7) == block) & ((row >> 3) == (column & 3))
    pick = pick.astype(F32)

    h2_wait(1)
    slab = (slab_all[0] + slab_all[1]).reshape(ROWS, 128)
    weights = slab_recv[:, :, 128:384].reshape(8 * NZ, ROWS)
    hole = jnp.dot(weights, slab, precision=lax.Precision.HIGHEST, preferred_element_type=F32)
    hole_send[...] = hole.reshape(NZ, 8, 128)
    for d in range(1, NZ):
        h3_copy(d).start()
    hole_recv[z] = hole_send[z]

    for way in range(2):
        wait_bytes(ring1.at[way], ring_sems.at[1, 1 + way])
    half_far = pl.ds(HALF * way_far, HALF)
    mine[to_far, half_far] += ring1[way_far]
    ring2_copy(way_far, to_far, half_far, ring_sems.at[1, 0]).start()
    mine[to_own, pl.ds(HALF * way_own, HALF)] += ring1[way_own]

    for g in range(PARTS):
        tiles = pl.ds(first(g), PART)
        core_copy(own, tiles, 1 + g).wait()
        for j in range(2):
            mine[2 * own + j, tiles] += got[2 * own + j, tiles]
        ring2_copy(way_own, to_own, tiles, late_sems.at[g]).start()
    wait_bytes(ring2.at[0], ring_sems.at[1, 0])
    for g in range(PARTS):
        tiles = pl.ds(first(g), PART)
        wait_bytes(ring2.at[0, tiles], late_sems.at[g])
        mine[x, tiles] += ring2[0, tiles] + ring2[1, tiles]

        for n in range(1 if g == PARTS - 1 else 0, PART):
            if g == PARTS - 1:
                to = first(g) + lax.rem(place - first(g) + n, PART)
            else:
                to = first(g) + n
            all_copy(to).start()
    recv[place] = mine[x, place]

    h3_wait(1)
    wait_bytes(recv.at[pl.ds(0, PLACES - 1)], all_sems.at[1])
    ladder = jnp.dot(
        pick,
        recv[...].reshape(PLACES * 8, 128),
        precision=lax.Precision.HIGHEST,
        preferred_element_type=F32,
    )
    for kk in range(4):
        total = driver[:, kk, :] + ladder[8 * kk : 8 * kk + 8]
        total += hole_recv[:, kk, :] + hole_recv[:, 4 + kk, :]
        below = vir_sum - occ_value[8 * kk : 8 * kk + 8] - occ_value[32 + 8 * kk : 40 + 8 * kk]
        out[:, kk, :] = total / below

    h1_wait(0)
    h2_wait(0)
    h3_wait(0)
    wait_bytes(recv.at[pl.ds(0, PLACES - 1)], all_sems.at[0])
    wait_bytes(mine.at[pl.ds(0, NX - 1)], ring_sems.at[0, 0])


def body(
    t2_packed,
    w_packed,
    pair_list,
    block_starts,
    singles,
    row_pairs,
    col_pairs,
    t2_slab,
    w_hole,
    driver,
    occ_energy,
    vir_energy,
):
    hbm = pl.BlockSpec(memory_space=pl.ANY)
    tiles = (NX, PLACES, 8, 128)
    return pl.pallas_call(
        ladder_kernel,
        out_shape=jax.ShapeDtypeStruct((GROUPS, 4, 128), F32),
        in_specs=[hbm] * 12,
        out_specs=pl.BlockSpec(memory_space=pltpu.VMEM),
        scratch_shapes=[
            pltpu.SMEM((GROUPS,), I32),
            pltpu.VMEM((OCC, VIRT), F32),
            pltpu.VMEM((2, PIECE), I32),
            pltpu.VMEM((GROUPS, 2, ROWS), I32),
            pltpu.VMEM((GROUPS, 2, 128), I32),
            pltpu.VMEM((GROUPS, 4, 128), F32),
            pltpu.VMEM((GROUPS, 4, ROWS), F32),
            pltpu.VMEM((GROUPS, 4, 128), F32),
            pltpu.VMEM((1, OCC), F32),
            pltpu.VMEM((1, VIRT), F32),
            pltpu.VMEM((CHUNKS, CHUNK, ROWS), F32),
            pltpu.VMEM((CHUNKS, CHUNK, COLS), F32),
            pltpu.VMEM((CHUNKS, CHUNK, 8), I32),
            pltpu.VMEM((128, 1024), F32),
            pltpu.VMEM((1024, 256), BF16),
            pltpu.VMEM((2, 2, 256, ROWS), BF16),
            pltpu.VMEM((ROWS, WIDE), F32),
            pltpu.VMEM((ROWS, WIDE), F32),
            pltpu.VMEM(tiles, F32),
            pltpu.VMEM(tiles, F32),
            pltpu.VMEM(tiles, F32),
            pltpu.VMEM((2, HALF, 8, 128), F32),
            pltpu.VMEM((2, PLACES, 8, 128), F32),
            pltpu.VMEM((PLACES, 8, 128), F32),
            pltpu.VMEM((2, CHUNKS, CHUNK, 256), BF16),
            pltpu.VMEM((CHUNKS + 1, CHUNK, ROWS), BF16),
            pltpu.VMEM((CHUNKS + 1, CHUNK, ROWS), BF16),
            pltpu.VMEM((NZ, 8, 384), F32),
            pltpu.VMEM((NZ, 8, 384), F32),
            pltpu.VMEM((2, NZ, NY, 8, 128), F32),
            pltpu.VMEM((NZ, 8, 128), F32),
            pltpu.VMEM((NZ, 8, 128), F32),
            pltpu.SemaphoreType.DMA((10,)),
            pltpu.SemaphoreType.DMA((2, CHUNKS)),
            pltpu.SemaphoreType.DMA((2, 1 + PARTS)),
            pltpu.SemaphoreType.DMA((2, 3)),
            pltpu.SemaphoreType.DMA((PARTS,)),
            pltpu.SemaphoreType.DMA((2,)),
            pltpu.SemaphoreType.DMA((2, 3)),
        ],
        compiler_params=pltpu.CompilerParams(
            collective_id=0, has_side_effects=True, vmem_limit_bytes=60 * 2**20
        ),
        name="ladder",
    )(
        block_starts,
        singles,
        pair_list,
        row_pairs.transpose(0, 2, 1),
        col_pairs.transpose(0, 2, 1),
        t2_slab,
        w_hole,
        driver,
        occ_energy.reshape(1, OCC),
        vir_energy.reshape(1, VIRT),
        t2_packed.T.reshape(CHUNKS, CHUNK, ROWS),
        w_packed.reshape(CHUNKS, CHUNK, COLS),
    )


def solution(mesh):
    in_specs = (
        P(None, ("virt", "rep")),
        P(("virt", "rep"), None),
        P(None, ("virt", "rep")),
        P(),
        P(),
        P(),
        P(None, "rep", None),
        P(None, "virt", "rep"),
        P(None, "virt", None),
        P(None, "virt", "rep"),
        P(),
        P(),
    )
    out_specs = P(None, "virt", "rep")
    return jax.shard_map(body, mesh=mesh, in_specs=in_specs, out_specs=out_specs, check_vma=False)
```

```python
import jax
import jax.numpy as jnp
from jax import lax
from jax.experimental import pallas as pl
from jax.experimental.pallas import tpu as pltpu
from jax.sharding import PartitionSpec as P

MESH = pl.DeviceIdType.MESH
F32 = jnp.float32
BF16 = jnp.bfloat16
I32 = jnp.int32

GROUPS = 8
OCC = 120
VIRT = 960
ROWS = 256
COLS = 512
PIECE = 3600
CHUNK = 720
CHUNKS = PIECE // CHUNK
WIDE = COLS // 2
NZ = 8
NY = 4
NX = 4
PLACES = NZ * NY
PLACE = 8 * PIECE
PARTS = 4
PART = PLACES // PARTS
HALF = PLACES // 2


def split(value):
    high = value.astype(BF16)
    return high, (value - high.astype(F32)).astype(BF16)


def block_at(starts, position):
    block = jnp.int32(0)
    for h in range(1, GROUPS):
        block += (position >= starts[h]).astype(I32)
    return block


def over_rows(left, right):
    return lax.dot_general(left, right, (((0,), (0,)), ((), ())), preferred_element_type=F32)


def lookup(columns, index):
    low = index & 127
    tile = index >> 7
    found = jnp.zeros((8, 128), F32)
    for t in range(8):
        piece = jnp.take_along_axis(
            columns[:, 128 * t : 128 * (t + 1)], low, axis=1, mode="promise_in_bounds"
        )
        found = jnp.where(tile == t, piece, found)
    return found


def ladder_kernel(
    starts_hbm,
    singles_hbm,
    pairs_hbm,
    rows_hbm,
    cols_hbm,
    slab_hbm,
    hole_hbm,
    driver_hbm,
    occ_hbm,
    vir_hbm,
    t2_hbm,
    w_hbm,
    out,
    starts,
    singles,
    pairs,
    rows,
    cols,
    t2_slab,
    w_hole,
    driver,
    occ,
    vir,
    t2,
    w,
    pair,
    padded,
    table,
    select,
    parts,
    mine,
    give,
    got,
    ring1,
    ring2,
    recv,
    orbits,
    d_high,
    d_low,
    slab_send,
    slab_recv,
    slab_all,
    hole_send,
    hole_recv,
    small_sems,
    load_sems,
    core_sems,
    ring_sems,
    late_sems,
    all_sems,
    hole_sems,
):
    virt = lax.axis_index("virt")
    x = lax.axis_index("rep")
    core = lax.rem(virt, 2)
    place = virt // 2
    y = lax.rem(place, NY)
    z = place // NY
    xp = lax.rem(x + 1, NX)
    xo = lax.rem(x + 2, NX)
    xm = lax.rem(x + 3, NX)

    small = [
        pltpu.make_async_copy(source, target, small_sems.at[n])
        for n, (source, target) in enumerate(
            (
                (starts_hbm, starts),
                (singles_hbm, singles),
                (pairs_hbm, pairs),
                (rows_hbm, rows),
                (cols_hbm, cols),
                (slab_hbm, t2_slab),
                (hole_hbm, w_hole),
                (driver_hbm, driver),
                (occ_hbm, occ),
                (vir_hbm, vir),
            )
        )
    ]
    for copy in small:
        copy.start()

    def load_t2(k):
        return pltpu.make_async_copy(t2_hbm.at[k], t2.at[k], load_sems.at[0, k])

    def load_w(k):
        return pltpu.make_async_copy(w_hbm.at[k], w.at[k], load_sems.at[1, k])

    load_t2(0).start()
    load_t2(1).start()

    def device(place_to, core_to):
        return (place_to * 2 + core_to, x)

    barrier = pltpu.get_barrier_semaphore()

    def greet(target):
        pl.semaphore_signal(barrier, inc=1, device_id=target, device_id_type=MESH)

    greet(device(place, 1 - core))
    greet((virt, xp))
    greet((virt, xm))

    for d in range(1, PLACES):
        greet(device(lax.rem(place + d, PLACES), core))
    for d in range(1, NY):
        greet(device(z * NY + lax.rem(y + d, NY), 1 - core))

    for copy in small:
        copy.wait()

    segment = virt * NX + x
    block_a = block_at(starts, place * PLACE)
    block_b = block_at(starts, place * PLACE + PLACE - 1)
    count = jnp.clip(starts[block_b] - segment * PIECE, 0, PIECE)
    mixed = jnp.minimum(count // CHUNK, CHUNKS - 1)
    padded[...] = jnp.zeros_like(padded)
    padded[0:OCC, 0:VIRT] = singles[...]
    high, low = split(padded[...].T)
    table[:, 0:128] = high
    table[:, 128:256] = low
    for k in range(CHUNKS):
        part = pairs[:, k * CHUNK : (k + 1) * CHUNK]
        pair[k] = jnp.concatenate([part, jnp.zeros((6, CHUNK), I32)], axis=0).T
    orbit = lax.broadcasted_iota(I32, (128, ROWS), 0)
    for s, block in enumerate((block_a, block_b)):
        for side in range(2):
            hit = (orbit == rows[block, side : side + 1, :]).astype(F32)
            select[s, side] = jnp.concatenate([hit, hit], axis=0).astype(BF16)

    row_index = []
    lane = lax.broadcasted_iota(I32, (GROUPS, ROWS), 1)
    for side in range(2):
        both = rows[:, side, :].astype(F32)
        for kk in range(4):
            hit = jnp.where(lane == virt * 4 + kk, both, 0.0)
            row_index.append(jnp.sum(hit, axis=1, keepdims=True).astype(I32))
    orbit = lax.broadcasted_iota(I32, (GROUPS, OCC), 1)
    hits = jnp.concatenate([(orbit == index).astype(F32) for index in row_index], axis=0)
    chosen = jnp.dot(hits, singles[...], precision=lax.Precision.HIGHEST, preferred_element_type=F32)
    chosen = jnp.concatenate([chosen, jnp.zeros((64, 64), F32)], axis=1)
    index_a = cols[:, 0, :]
    index_b = cols[:, 1, :]
    for kk in range(4):
        left = lookup(chosen[8 * kk : 8 * kk + 8], index_a)
        right = lookup(chosen[32 + 8 * kk : 40 + 8 * kk], index_b)
        value = t2_slab[:, kk, :] + left * right
        slab_send[:, kk, 0:128] = jnp.where(core == 0, value, 0.0)
        slab_send[:, 4 + kk, 0:128] = jnp.where(core == 0, 0.0, value)
        value = w_hole[:, kk, :]
        slab_send[:, kk, 128:384] = jnp.where(core == 0, value, 0.0)
        slab_send[:, 4 + kk, 128:384] = jnp.where(core == 0, 0.0, value)

    def gathered(index):
        hit = (lax.broadcasted_iota(I32, (index.shape[0], 1024), 1) == index).astype(BF16)
        return jnp.dot(hit, table[...], preferred_element_type=F32).astype(BF16)

    def dressed(k, select_i, select_j):
        left = jnp.dot(orbits[0, k], select_i, preferred_element_type=F32)
        right = jnp.dot(orbits[1, k], select_j, preferred_element_type=F32)
        return t2[k] + left * right

    in_chunk = lax.broadcasted_iota(I32, (CHUNK, ROWS), 0)

    def dress(k):
        if k + 2 < CHUNKS:
            load_t2(k + 2).start()
        load_w(k).start()
        load_t2(k).wait()
        index = pair[k]
        orbits[0, k] = gathered(index[:, 0:1])
        orbits[1, k] = gathered(index[:, 1:2])
        in_a = k <= mixed
        value = dressed(
            k,
            jnp.where(in_a, select[0, 0], select[1, 0]),
            jnp.where(in_a, select[0, 1], select[1, 1]),
        )
        bound = jnp.where(k > mixed, CHUNK, count - k * CHUNK)
        d_high[k], d_low[k] = split(jnp.where(in_chunk < bound, value, 0.0))

    def dress_rest():
        value = dressed(mixed, select[1, 0], select[1, 1])
        value = jnp.where(in_chunk < count - mixed * CHUNK, 0.0, value)
        d_high[CHUNKS], d_low[CHUNKS] = split(value)

    def product(k, n, half):
        columns = pl.ds(pl.multiple_of(half * WIDE, WIDE), WIDE)
        w_high, w_low = split(w[n, :, columns])
        return (
            over_rows(d_high[k], w_high) + over_rows(d_high[k], w_low) + over_rows(d_low[k], w_high)
        )

    def multiply(k, half):
        parts[k] = product(k, k, half)

    def sums(rows_of, columns):
        a = jnp.zeros((8 * PART, 128), F32)
        b = parts[CHUNKS, rows_of, columns]
        for k in range(CHUNKS):
            part = parts[k, rows_of, columns]
            a += part * jnp.where(k <= mixed, 1.0, 0.0)
            b += part * jnp.where(k > mixed, 1.0, 0.0)
        return a.reshape(PART, 8, 128), b.reshape(PART, 8, 128)

    def h1_copy(d):
        to = lax.rem(z + d, NZ)
        return pltpu.make_async_remote_copy(
            src_ref=slab_send.at[to],
            dst_ref=slab_recv.at[z],
            send_sem=hole_sems.at[0, 0],
            recv_sem=hole_sems.at[1, 0],
            device_id=device(to * NY + y, core),
            device_id_type=MESH,
        )

    def h2_copy(d):
        other = lax.rem(y * 2 + core + d, 2 * NY)
        return pltpu.make_async_remote_copy(
            src_ref=slab_recv.at[:, :, pl.ds(0, 128)],
            dst_ref=slab_all.at[core, :, y],
            send_sem=hole_sems.at[0, 1],
            recv_sem=hole_sems.at[1, 1],
            device_id=(z * 2 * NY + other, x),
            device_id_type=MESH,
        )

    def h3_copy(d):
        to = lax.rem(z + d, NZ)
        return pltpu.make_async_remote_copy(
            src_ref=hole_send.at[to],
            dst_ref=hole_recv.at[z],
            send_sem=hole_sems.at[0, 2],
            recv_sem=hole_sems.at[1, 2],
            device_id=device(to * NY + y, core),
            device_id_type=MESH,
        )

    def wait_bytes(ref, sem):
        pltpu.make_async_copy(ref, ref, sem).wait()

    def h1_wait(end):
        wait_bytes(slab_recv.at[pl.ds(0, NZ - 1)], hole_sems.at[end, 0])

    def h2_wait(end):
        wait_bytes(slab_all.at[:, pl.ds(0, NZ - 1)], hole_sems.at[end, 1])

    def h3_wait(end):
        wait_bytes(hole_recv.at[pl.ds(0, NZ - 1)], hole_sems.at[end, 2])

    own = x // 2
    far = 1 - own
    odd = lax.rem(x, 2)
    way_far = 1 - odd
    way_own = odd
    to_far = jnp.where(odd == 0, xm, xp)
    to_own = jnp.where(odd == 0, xp, xm)

    def first(g):
        return lax.rem(z // 2 + 1 + g, PARTS) * PART

    def core_copy(half, tiles, n):
        part = (pl.ds(2 * half, 2), tiles)
        return pltpu.make_async_remote_copy(
            src_ref=give.at[part],
            dst_ref=got.at[part],
            send_sem=core_sems.at[0, n],
            recv_sem=core_sems.at[1, n],
            device_id=device(place, 1 - core),
            device_id_type=MESH,
        )

    def ring1_copy(way):
        return pltpu.make_async_remote_copy(
            src_ref=mine.at[xo, pl.ds(HALF * way, HALF)],
            dst_ref=ring1.at[way],
            send_sem=ring_sems.at[0, 0],
            recv_sem=ring_sems.at[1, 1 + way],
            device_id=(virt, xp if way == 0 else xm),
            device_id_type=MESH,
        )

    def ring2_copy(way, to, tiles, recv_sem):
        return pltpu.make_async_remote_copy(
            src_ref=mine.at[to, tiles],
            dst_ref=ring2.at[way, tiles],
            send_sem=ring_sems.at[0, 0],
            recv_sem=recv_sem,
            device_id=(virt, to),
            device_id_type=MESH,
        )

    def all_copy(to):
        return pltpu.make_async_remote_copy(
            src_ref=mine.at[x, to],
            dst_ref=recv.at[place],
            send_sem=all_sems.at[0],
            recv_sem=all_sems.at[1],
            device_id=device(to, core),
            device_id_type=MESH,
        )

    upper = lax.broadcasted_iota(I32, (PART, 8, 128), 1) < 4

    def assemble(half, g):
        rows_of = pl.ds(pl.multiple_of(first(g) * 8, 8 * PART), 8 * PART)
        tiles = pl.ds(first(g), PART)
        for j in range(2):
            a, b = sums(rows_of, slice(128 * j, 128 * (j + 1)))
            tile0 = jnp.where(upper, a, pltpu.roll(b, 4, 1))
            tile1 = jnp.where(upper, pltpu.roll(a, 4, 1), b)
            mine[2 * half + j, tiles] = jnp.where(core == 0, tile0, tile1)
            give[2 * half + j, tiles] = jnp.where(core == 0, tile1, tile0)

    everything = pl.ds(0, PLACES)

    for k in range(CHUNKS):
        dress(k)
    dress_rest()
    pl.semaphore_wait(barrier, 2 + PLACES - 1 + 1 + NY - 1)
    for d in range(1, NZ):
        h1_copy(d).start()
    slab_recv[z] = slab_send[z]

    for k in range(CHUNKS):
        load_w(k).wait()
    for k in range(CHUNKS):
        multiply(k, far)
    parts[CHUNKS] = product(CHUNKS, mixed, far)
    for g in range(PARTS):
        assemble(far, g)
    core_copy(far, everything, 0).start()

    h1_wait(1)
    for d in range(1, 2 * NY):
        h2_copy(d).start()
    slab_all[core, :, y] = slab_recv[:, :, 0:128]

    multiply(0, own)
    multiply(1, own)
    core_copy(far, everything, 0).wait()
    for j in range(2):
        mine[2 * far + j] += got[2 * far + j]
    for way in range(2):
        ring1_copy(way).start()
    ring2_copy(way_far, to_far, pl.ds(HALF * (1 - way_far), HALF), ring_sems.at[1, 0]).start()
    multiply(2, own)
    multiply(3, own)
    multiply(4, own)
    parts[CHUNKS] = product(CHUNKS, mixed, own)
    for g in range(PARTS):
        assemble(own, g)
        core_copy(own, pl.ds(first(g), PART), 1 + g).start()

    for way in range(2):
        wait_bytes(ring1.at[way], ring_sems.at[1, 1 + way])
    half_far = pl.ds(HALF * way_far, HALF)
    mine[to_far, half_far] += ring1[way_far]
    ring2_copy(way_far, to_far, half_far, ring_sems.at[1, 0]).start()
    mine[to_own, pl.ds(HALF * way_own, HALF)] += ring1[way_own]

    for g in range(PARTS):
        tiles = pl.ds(first(g), PART)
        core_copy(own, tiles, 1 + g).wait()
        for j in range(2):
            mine[2 * own + j, tiles] += got[2 * own + j, tiles]
        ring2_copy(way_own, to_own, tiles, late_sems.at[g]).start()
    h2_wait(1)
    slab = (slab_all[0] + slab_all[1]).reshape(ROWS, 128)
    weights = slab_recv[:, :, 128:384].reshape(8 * NZ, ROWS)
    hole = jnp.dot(weights, slab, precision=lax.Precision.HIGHEST, preferred_element_type=F32)
    hole_send[...] = hole.reshape(NZ, 8, 128)
    for d in range(1, NZ):
        h3_copy(d).start()
    hole_recv[z] = hole_send[z]

    wait_bytes(ring2.at[0], ring_sems.at[1, 0])
    for g in range(PARTS):
        tiles = pl.ds(first(g), PART)
        wait_bytes(ring2.at[0, tiles], late_sems.at[g])
        mine[x, tiles] += ring2[0, tiles] + ring2[1, tiles]

        for n in range(1 if g == PARTS - 1 else 0, PART):
            if g == PARTS - 1:
                to = first(g) + lax.rem(place - first(g) + n, PART)
            else:
                to = first(g) + n
            all_copy(to).start()
    recv[place] = mine[x, place]

    zeros = jnp.zeros((8, 64), F32)
    energy = jnp.concatenate([jnp.broadcast_to(vir[...], (8, VIRT)), zeros], axis=1)
    vir_sum = lookup(energy, index_a) + lookup(energy, index_b)
    occ_value = jnp.sum(hits * occ[...], axis=1, keepdims=True)
    column = lax.broadcasted_iota(I32, (32, PLACES * 8), 1)
    row = lax.broadcasted_iota(I32, (32, PLACES * 8), 0)
    position = (column >> 3) * PLACE + ((column >> 2) & 1) * (PLACE - 1)
    block = jnp.zeros_like(column)
    for h in range(1, GROUPS):
        block += (position >= starts[h]).astype(I32)
    pick = ((row & 7) == block) & ((row >> 3) == (column & 3))
    pick = pick.astype(F32).astype(BF16)

    h3_wait(1)
    wait_bytes(recv.at[pl.ds(0, PLACES - 1)], all_sems.at[1])
    tiles = recv[...].reshape(PLACES * 8, 128)
    high = tiles.astype(BF16)
    rest = tiles - high.astype(F32)
    middle, low = split(rest)
    ladder = jnp.dot(pick, low, preferred_element_type=F32)
    ladder += jnp.dot(pick, middle, preferred_element_type=F32)
    ladder += jnp.dot(pick, high, preferred_element_type=F32)
    for kk in range(4):
        total = driver[:, kk, :] + ladder[8 * kk : 8 * kk + 8]
        total += hole_recv[:, kk, :] + hole_recv[:, 4 + kk, :]
        below = vir_sum - occ_value[8 * kk : 8 * kk + 8] - occ_value[32 + 8 * kk : 40 + 8 * kk]
        out[:, kk, :] = total / below

    h1_wait(0)
    h2_wait(0)
    h3_wait(0)
    wait_bytes(recv.at[pl.ds(0, PLACES - 1)], all_sems.at[0])
    wait_bytes(mine.at[pl.ds(0, NX - 1)], ring_sems.at[0, 0])


def body(
    t2_packed,
    w_packed,
    pair_list,
    block_starts,
    singles,
    row_pairs,
    col_pairs,
    t2_slab,
    w_hole,
    driver,
    occ_energy,
    vir_energy,
):
    hbm = pl.BlockSpec(memory_space=pl.ANY)
    tiles = (NX, PLACES, 8, 128)
    return pl.pallas_call(
        ladder_kernel,
        out_shape=pltpu.VMEM((GROUPS, 4, 128), F32),
        in_specs=[hbm] * 12,
        out_specs=pl.BlockSpec(memory_space=pltpu.VMEM),
        scratch_shapes=[
            pltpu.SMEM((GROUPS,), I32),
            pltpu.VMEM((OCC, VIRT), F32),
            pltpu.VMEM((2, PIECE), I32),
            pltpu.VMEM((GROUPS, 2, ROWS), I32),
            pltpu.VMEM((GROUPS, 2, 128), I32),
            pltpu.VMEM((GROUPS, 4, 128), F32),
            pltpu.VMEM((GROUPS, 4, ROWS), F32),
            pltpu.VMEM((GROUPS, 4, 128), F32),
            pltpu.VMEM((1, OCC), F32),
            pltpu.VMEM((1, VIRT), F32),
            pltpu.VMEM((CHUNKS, CHUNK, ROWS), F32),
            pltpu.VMEM((CHUNKS, CHUNK, COLS), F32),
            pltpu.VMEM((CHUNKS, CHUNK, 8), I32),
            pltpu.VMEM((128, 1024), F32),
            pltpu.VMEM((1024, 256), BF16),
            pltpu.VMEM((2, 2, 256, ROWS), BF16),
            pltpu.VMEM((CHUNKS + 1, ROWS, WIDE), F32),
            pltpu.VMEM(tiles, F32),
            pltpu.VMEM(tiles, F32),
            pltpu.VMEM(tiles, F32),
            pltpu.VMEM((2, HALF, 8, 128), F32),
            pltpu.VMEM((2, PLACES, 8, 128), F32),
            pltpu.VMEM((PLACES, 8, 128), F32),
            pltpu.VMEM((2, CHUNKS, CHUNK, 256), BF16),
            pltpu.VMEM((CHUNKS + 1, CHUNK, ROWS), BF16),
            pltpu.VMEM((CHUNKS + 1, CHUNK, ROWS), BF16),
            pltpu.VMEM((NZ, 8, 384), F32),
            pltpu.VMEM((NZ, 8, 384), F32),
            pltpu.VMEM((2, NZ, NY, 8, 128), F32),
            pltpu.VMEM((NZ, 8, 128), F32),
            pltpu.VMEM((NZ, 8, 128), F32),
            pltpu.SemaphoreType.DMA((10,)),
            pltpu.SemaphoreType.DMA((2, CHUNKS)),
            pltpu.SemaphoreType.DMA((2, 1 + PARTS)),
            pltpu.SemaphoreType.DMA((2, 3)),
            pltpu.SemaphoreType.DMA((PARTS,)),
            pltpu.SemaphoreType.DMA((2,)),
            pltpu.SemaphoreType.DMA((2, 3)),
        ],
        compiler_params=pltpu.CompilerParams(
            collective_id=0, has_side_effects=True, vmem_limit_bytes=60 * 2**20
        ),
        name="ladder",
    )(
        block_starts,
        singles,
        pair_list,
        row_pairs.transpose(0, 2, 1),
        col_pairs.transpose(0, 2, 1),
        t2_slab,
        w_hole,
        driver,
        occ_energy.reshape(1, OCC),
        vir_energy.reshape(1, VIRT),
        t2_packed.T.reshape(CHUNKS, CHUNK, ROWS),
        w_packed.reshape(CHUNKS, CHUNK, COLS),
    )


def solution(mesh):
    in_specs = (
        P(None, ("virt", "rep")),
        P(("virt", "rep"), None),
        P(None, ("virt", "rep")),
        P(),
        P(),
        P(),
        P(None, "rep", None),
        P(None, "virt", "rep"),
        P(None, "virt", None),
        P(None, "virt", "rep"),
        P(),
        P(),
    )
    out_specs = P(None, "virt", "rep")
    return jax.shard_map(body, mesh=mesh, in_specs=in_specs, out_specs=out_specs, check_vma=False)
```

```python
import jax
import jax.numpy as jnp
from jax import lax
from jax.experimental import pallas as pl
from jax.experimental.pallas import tpu as pltpu
from jax.sharding import PartitionSpec as P

MESH = pl.DeviceIdType.MESH
F32 = jnp.float32
BF16 = jnp.bfloat16
I32 = jnp.int32

GROUPS = 8
OCC = 120
VIRT = 960
ROWS = 256
COLS = 512
PIECE = 3600
CHUNK = 720
CHUNKS = PIECE // CHUNK
WIDE = COLS // 2
NZ = 8
NY = 4
NX = 4
PLACES = NZ * NY
PLACE = 8 * PIECE
PARTS = 4
PART = PLACES // PARTS
HALF = PLACES // 2


def split(value):
    high = value.astype(BF16)
    return high, (value - high.astype(F32)).astype(BF16)


def block_at(starts, position):
    block = jnp.int32(0)
    for h in range(1, GROUPS):
        block += (position >= starts[h]).astype(I32)
    return block


def over_rows(left, right):
    return lax.dot_general(left, right, (((0,), (0,)), ((), ())), preferred_element_type=F32)


def lookup(columns, index):
    low = index & 127
    tile = index >> 7
    found = jnp.zeros((8, 128), F32)
    for t in range(8):
        piece = jnp.take_along_axis(
            columns[:, 128 * t : 128 * (t + 1)], low, axis=1, mode="promise_in_bounds"
        )
        found = jnp.where(tile == t, piece, found)
    return found


def ladder_kernel(
    starts_hbm,
    singles_hbm,
    pairs_hbm,
    rows_hbm,
    cols_hbm,
    slab_hbm,
    hole_hbm,
    driver_hbm,
    occ_hbm,
    vir_hbm,
    t2_hbm,
    w_hbm,
    out,
    starts,
    singles,
    pairs,
    rows,
    cols,
    t2_slab,
    w_hole,
    driver,
    occ,
    vir,
    t2,
    w,
    pair,
    padded,
    table,
    select,
    parts,
    mine,
    give,
    got,
    ring1,
    ring2,
    recv,
    orbits,
    d_high,
    d_low,
    slab_send,
    slab_recv,
    slab_all,
    hole_send,
    hole_recv,
    small_sems,
    load_sems,
    core_sems,
    ring_sems,
    late_sems,
    all_sems,
    hole_sems,
):
    virt = lax.axis_index("virt")
    x = lax.axis_index("rep")
    core = lax.rem(virt, 2)
    place = virt // 2
    y = lax.rem(place, NY)
    z = place // NY
    xp = lax.rem(x + 1, NX)
    xo = lax.rem(x + 2, NX)
    xm = lax.rem(x + 3, NX)

    small = [
        pltpu.make_async_copy(source, target, small_sems.at[n])
        for n, (source, target) in enumerate(
            (
                (starts_hbm, starts),
                (singles_hbm, singles),
                (pairs_hbm, pairs),
                (rows_hbm, rows),
                (cols_hbm, cols),
                (slab_hbm, t2_slab),
                (hole_hbm, w_hole),
                (driver_hbm, driver),
                (occ_hbm, occ),
                (vir_hbm, vir),
            )
        )
    ]
    for copy in small[:4]:
        copy.start()

    def load_t2(k):
        return pltpu.make_async_copy(t2_hbm.at[k], t2.at[k], load_sems.at[0, k])

    def load_w(k):
        return pltpu.make_async_copy(w_hbm.at[k], w.at[k], load_sems.at[1, k])

    load_t2(0).start()
    for copy in small[4:]:
        copy.start()
    load_t2(1).start()

    def device(place_to, core_to):
        return (place_to * 2 + core_to, x)

    barrier = pltpu.get_barrier_semaphore()

    def greet(target):
        pl.semaphore_signal(barrier, inc=1, device_id=target, device_id_type=MESH)

    greet(device(place, 1 - core))
    greet((virt, xp))
    greet((virt, xm))

    for d in range(1, PLACES):
        greet(device(lax.rem(place + d, PLACES), core))
    for d in range(1, NY):
        greet(device(z * NY + lax.rem(y + d, NY), 1 - core))

    for copy in small[:4]:
        copy.wait()

    segment = virt * NX + x
    block_a = block_at(starts, place * PLACE)
    block_b = block_at(starts, place * PLACE + PLACE - 1)
    count = jnp.clip(starts[block_b] - segment * PIECE, 0, PIECE)
    mixed = jnp.minimum(count // CHUNK, CHUNKS - 1)
    padded[...] = jnp.zeros_like(padded)
    padded[0:OCC, 0:VIRT] = singles[...]
    high, low = split(padded[...].T)
    table[:, 0:128] = high
    table[:, 128:256] = low
    for k in range(CHUNKS):
        part = pairs[:, k * CHUNK : (k + 1) * CHUNK]
        pair[k] = jnp.concatenate([part, jnp.zeros((6, CHUNK), I32)], axis=0).T
    orbit = lax.broadcasted_iota(I32, (128, ROWS), 0)
    for s, block in enumerate((block_a, block_b)):
        for side in range(2):
            hit = (orbit == rows[block, side : side + 1, :]).astype(F32)
            select[s, side] = jnp.concatenate([hit, hit], axis=0).astype(BF16)

    def gathered(index):
        hit = (lax.broadcasted_iota(I32, (index.shape[0], 1024), 1) == index).astype(BF16)
        return jnp.dot(hit, table[...], preferred_element_type=F32).astype(BF16)

    def dressed(k, select_i, select_j):
        left = jnp.dot(orbits[0, k], select_i, preferred_element_type=F32)
        right = jnp.dot(orbits[1, k], select_j, preferred_element_type=F32)
        return t2[k] + left * right

    in_chunk = lax.broadcasted_iota(I32, (CHUNK, ROWS), 0)

    def dress(k):
        if k + 2 < CHUNKS:
            load_t2(k + 2).start()
        load_w(k).start()
        load_t2(k).wait()
        index = pair[k]
        orbits[0, k] = gathered(index[:, 0:1])
        orbits[1, k] = gathered(index[:, 1:2])
        in_a = k <= mixed
        value = dressed(
            k,
            jnp.where(in_a, select[0, 0], select[1, 0]),
            jnp.where(in_a, select[0, 1], select[1, 1]),
        )
        bound = jnp.where(k > mixed, CHUNK, count - k * CHUNK)
        d_high[k], d_low[k] = split(jnp.where(in_chunk < bound, value, 0.0))

    def dress_rest():
        value = dressed(mixed, select[1, 0], select[1, 1])
        value = jnp.where(in_chunk < count - mixed * CHUNK, 0.0, value)
        d_high[CHUNKS], d_low[CHUNKS] = split(value)

    def product(k, n, half):
        columns = pl.ds(pl.multiple_of(half * WIDE, WIDE), WIDE)
        w_high, w_low = split(w[n, :, columns])
        return (
            over_rows(d_high[k], w_high) + over_rows(d_high[k], w_low) + over_rows(d_low[k], w_high)
        )

    def multiply(k, half):
        parts[k] = product(k, k, half)

    def sums(rows_of, columns):
        a = jnp.zeros((8 * PART, 128), F32)
        b = parts[CHUNKS, rows_of, columns]
        for k in range(CHUNKS):
            part = parts[k, rows_of, columns]
            a += part * jnp.where(k <= mixed, 1.0, 0.0)
            b += part * jnp.where(k > mixed, 1.0, 0.0)
        return a.reshape(PART, 8, 128), b.reshape(PART, 8, 128)

    def h1_copy(d):
        to = lax.rem(z + d, NZ)
        return pltpu.make_async_remote_copy(
            src_ref=slab_send.at[to],
            dst_ref=slab_recv.at[z],
            send_sem=hole_sems.at[0, 0],
            recv_sem=hole_sems.at[1, 0],
            device_id=device(to * NY + y, core),
            device_id_type=MESH,
        )

    def h2_copy(d):
        other = lax.rem(y * 2 + core + d, 2 * NY)
        return pltpu.make_async_remote_copy(
            src_ref=slab_recv.at[:, :, pl.ds(0, 128)],
            dst_ref=slab_all.at[core, :, y],
            send_sem=hole_sems.at[0, 1],
            recv_sem=hole_sems.at[1, 1],
            device_id=(z * 2 * NY + other, x),
            device_id_type=MESH,
        )

    def h3_copy(d):
        to = lax.rem(z + d, NZ)
        return pltpu.make_async_remote_copy(
            src_ref=hole_send.at[to],
            dst_ref=hole_recv.at[z],
            send_sem=hole_sems.at[0, 2],
            recv_sem=hole_sems.at[1, 2],
            device_id=device(to * NY + y, core),
            device_id_type=MESH,
        )

    def wait_bytes(ref, sem):
        pltpu.make_async_copy(ref, ref, sem).wait()

    def h1_wait(end):
        wait_bytes(slab_recv.at[pl.ds(0, NZ - 1)], hole_sems.at[end, 0])

    def h2_wait(end):
        wait_bytes(slab_all.at[:, pl.ds(0, NZ - 1)], hole_sems.at[end, 1])

    def h3_wait(end):
        wait_bytes(hole_recv.at[pl.ds(0, NZ - 1)], hole_sems.at[end, 2])

    own = x // 2
    far = 1 - own
    odd = lax.rem(x, 2)
    way_far = 1 - odd
    way_own = odd
    to_far = jnp.where(odd == 0, xm, xp)
    to_own = jnp.where(odd == 0, xp, xm)

    def first(g):
        return lax.rem(z // 2 + 1 + g, PARTS) * PART

    def core_copy(half, tiles, n):
        part = (pl.ds(2 * half, 2), tiles)
        return pltpu.make_async_remote_copy(
            src_ref=give.at[part],
            dst_ref=got.at[part],
            send_sem=core_sems.at[0, n],
            recv_sem=core_sems.at[1, n],
            device_id=device(place, 1 - core),
            device_id_type=MESH,
        )

    def ring1_copy(way):
        return pltpu.make_async_remote_copy(
            src_ref=mine.at[xo, pl.ds(HALF * way, HALF)],
            dst_ref=ring1.at[way],
            send_sem=ring_sems.at[0, 0],
            recv_sem=ring_sems.at[1, 1 + way],
            device_id=(virt, xp if way == 0 else xm),
            device_id_type=MESH,
        )

    def ring2_copy(way, to, tiles, recv_sem):
        return pltpu.make_async_remote_copy(
            src_ref=mine.at[to, tiles],
            dst_ref=ring2.at[way, tiles],
            send_sem=ring_sems.at[0, 0],
            recv_sem=recv_sem,
            device_id=(virt, to),
            device_id_type=MESH,
        )

    def all_copy(to):
        return pltpu.make_async_remote_copy(
            src_ref=mine.at[x, to],
            dst_ref=recv.at[place],
            send_sem=all_sems.at[0],
            recv_sem=all_sems.at[1],
            device_id=device(to, core),
            device_id_type=MESH,
        )

    upper = lax.broadcasted_iota(I32, (PART, 8, 128), 1) < 4

    def assemble(half, g):
        rows_of = pl.ds(pl.multiple_of(first(g) * 8, 8 * PART), 8 * PART)
        tiles = pl.ds(first(g), PART)
        for j in range(2):
            a, b = sums(rows_of, slice(128 * j, 128 * (j + 1)))
            tile0 = jnp.where(upper, a, pltpu.roll(b, 4, 1))
            tile1 = jnp.where(upper, pltpu.roll(a, 4, 1), b)
            mine[2 * half + j, tiles] = jnp.where(core == 0, tile0, tile1)
            give[2 * half + j, tiles] = jnp.where(core == 0, tile1, tile0)

    everything = pl.ds(0, PLACES)

    for k in range(CHUNKS):
        dress(k)
    dress_rest()

    for copy in small[4:]:
        copy.wait()

    row_index = []
    lane = lax.broadcasted_iota(I32, (GROUPS, ROWS), 1)
    for side in range(2):
        both = rows[:, side, :].astype(F32)
        for kk in range(4):
            hit = jnp.where(lane == virt * 4 + kk, both, 0.0)
            row_index.append(jnp.sum(hit, axis=1, keepdims=True).astype(I32))
    orbit = lax.broadcasted_iota(I32, (GROUPS, OCC), 1)
    hits = jnp.concatenate([(orbit == index).astype(F32) for index in row_index], axis=0)
    chosen = jnp.dot(hits, singles[...], precision=lax.Precision.HIGHEST, preferred_element_type=F32)
    chosen = jnp.concatenate([chosen, jnp.zeros((64, 64), F32)], axis=1)
    index_a = cols[:, 0, :]
    index_b = cols[:, 1, :]
    for kk in range(4):
        left = lookup(chosen[8 * kk : 8 * kk + 8], index_a)
        right = lookup(chosen[32 + 8 * kk : 40 + 8 * kk], index_b)
        value = t2_slab[:, kk, :] + left * right
        slab_send[:, kk, 0:128] = jnp.where(core == 0, value, 0.0)
        slab_send[:, 4 + kk, 0:128] = jnp.where(core == 0, 0.0, value)
        value = w_hole[:, kk, :]
        slab_send[:, kk, 128:384] = jnp.where(core == 0, value, 0.0)
        slab_send[:, 4 + kk, 128:384] = jnp.where(core == 0, 0.0, value)

    pl.semaphore_wait(barrier, 2 + PLACES - 1 + 1 + NY - 1)
    for d in range(1, NZ):
        h1_copy(d).start()
    slab_recv[z] = slab_send[z]

    for k in range(CHUNKS):
        load_w(k).wait()
    for k in range(CHUNKS):
        multiply(k, far)
    parts[CHUNKS] = product(CHUNKS, mixed, far)
    for g in range(PARTS):
        assemble(far, g)
    core_copy(far, everything, 0).start()

    h1_wait(1)
    for d in range(1, 2 * NY):
        h2_copy(d).start()
    slab_all[core, :, y] = slab_recv[:, :, 0:128]

    multiply(0, own)
    multiply(1, own)
    core_copy(far, everything, 0).wait()
    for j in range(2):
        mine[2 * far + j] += got[2 * far + j]
    for way in range(2):
        ring1_copy(way).start()
    ring2_copy(way_far, to_far, pl.ds(HALF * (1 - way_far), HALF), ring_sems.at[1, 0]).start()
    multiply(2, own)
    multiply(3, own)
    multiply(4, own)
    parts[CHUNKS] = product(CHUNKS, mixed, own)
    for g in range(PARTS):
        assemble(own, g)
        core_copy(own, pl.ds(first(g), PART), 1 + g).start()

    for way in range(2):
        wait_bytes(ring1.at[way], ring_sems.at[1, 1 + way])
    half_far = pl.ds(HALF * way_far, HALF)
    mine[to_far, half_far] += ring1[way_far]
    ring2_copy(way_far, to_far, half_far, ring_sems.at[1, 0]).start()
    mine[to_own, pl.ds(HALF * way_own, HALF)] += ring1[way_own]

    for g in range(PARTS):
        tiles = pl.ds(first(g), PART)
        core_copy(own, tiles, 1 + g).wait()
        for j in range(2):
            mine[2 * own + j, tiles] += got[2 * own + j, tiles]
        ring2_copy(way_own, to_own, tiles, late_sems.at[g]).start()
    h2_wait(1)
    slab = (slab_all[0] + slab_all[1]).reshape(ROWS, 128)
    weights = slab_recv[:, :, 128:384].reshape(8 * NZ, ROWS)
    hole = jnp.dot(weights, slab, precision=lax.Precision.HIGHEST, preferred_element_type=F32)
    hole_send[...] = hole.reshape(NZ, 8, 128)
    for d in range(1, NZ):
        h3_copy(d).start()
    hole_recv[z] = hole_send[z]

    wait_bytes(ring2.at[0], ring_sems.at[1, 0])
    for g in range(PARTS):
        tiles = pl.ds(first(g), PART)
        wait_bytes(ring2.at[0, tiles], late_sems.at[g])
        mine[x, tiles] += ring2[0, tiles] + ring2[1, tiles]

        for n in range(1 if g == PARTS - 1 else 0, PART):
            if g == PARTS - 1:
                to = first(g) + lax.rem(place - first(g) + n, PART)
            else:
                to = first(g) + n
            all_copy(to).start()
    recv[place] = mine[x, place]

    zeros = jnp.zeros((8, 64), F32)
    energy = jnp.concatenate([jnp.broadcast_to(vir[...], (8, VIRT)), zeros], axis=1)
    vir_sum = lookup(energy, index_a) + lookup(energy, index_b)
    occ_value = jnp.sum(hits * occ[...], axis=1, keepdims=True)
    column = lax.broadcasted_iota(I32, (32, PLACES * 8), 1)
    row = lax.broadcasted_iota(I32, (32, PLACES * 8), 0)
    position = (column >> 3) * PLACE + ((column >> 2) & 1) * (PLACE - 1)
    block = jnp.zeros_like(column)
    for h in range(1, GROUPS):
        block += (position >= starts[h]).astype(I32)
    pick = ((row & 7) == block) & ((row >> 3) == (column & 3))
    pick = pick.astype(F32).astype(BF16)

    h3_wait(1)
    wait_bytes(recv.at[pl.ds(0, PLACES - 1)], all_sems.at[1])
    tiles = recv[...].reshape(PLACES * 8, 128)
    high = tiles.astype(BF16)
    rest = tiles - high.astype(F32)
    middle, low = split(rest)
    ladder = jnp.dot(pick, low, preferred_element_type=F32)
    ladder += jnp.dot(pick, middle, preferred_element_type=F32)
    ladder += jnp.dot(pick, high, preferred_element_type=F32)
    for kk in range(4):
        total = driver[:, kk, :] + ladder[8 * kk : 8 * kk + 8]
        total += hole_recv[:, kk, :] + hole_recv[:, 4 + kk, :]
        below = vir_sum - occ_value[8 * kk : 8 * kk + 8] - occ_value[32 + 8 * kk : 40 + 8 * kk]
        out[:, kk, :] = total / below

    h1_wait(0)
    h2_wait(0)
    h3_wait(0)
    wait_bytes(recv.at[pl.ds(0, PLACES - 1)], all_sems.at[0])
    wait_bytes(mine.at[pl.ds(0, NX - 1)], ring_sems.at[0, 0])


def body(
    t2_packed,
    w_packed,
    pair_list,
    block_starts,
    singles,
    row_pairs,
    col_pairs,
    t2_slab,
    w_hole,
    driver,
    occ_energy,
    vir_energy,
):
    hbm = pl.BlockSpec(memory_space=pl.ANY)
    tiles = (NX, PLACES, 8, 128)
    return pl.pallas_call(
        ladder_kernel,
        out_shape=pltpu.VMEM((GROUPS, 4, 128), F32),
        in_specs=[hbm] * 12,
        out_specs=pl.BlockSpec(memory_space=pltpu.VMEM),
        scratch_shapes=[
            pltpu.SMEM((GROUPS,), I32),
            pltpu.VMEM((OCC, VIRT), F32),
            pltpu.VMEM((2, PIECE), I32),
            pltpu.VMEM((GROUPS, 2, ROWS), I32),
            pltpu.VMEM((GROUPS, 2, 128), I32),
            pltpu.VMEM((GROUPS, 4, 128), F32),
            pltpu.VMEM((GROUPS, 4, ROWS), F32),
            pltpu.VMEM((GROUPS, 4, 128), F32),
            pltpu.VMEM((1, OCC), F32),
            pltpu.VMEM((1, VIRT), F32),
            pltpu.VMEM((CHUNKS, CHUNK, ROWS), F32),
            pltpu.VMEM((CHUNKS, CHUNK, COLS), F32),
            pltpu.VMEM((CHUNKS, CHUNK, 8), I32),
            pltpu.VMEM((128, 1024), F32),
            pltpu.VMEM((1024, 256), BF16),
            pltpu.VMEM((2, 2, 256, ROWS), BF16),
            pltpu.VMEM((CHUNKS + 1, ROWS, WIDE), F32),
            pltpu.VMEM(tiles, F32),
            pltpu.VMEM(tiles, F32),
            pltpu.VMEM(tiles, F32),
            pltpu.VMEM((2, HALF, 8, 128), F32),
            pltpu.VMEM((2, PLACES, 8, 128), F32),
            pltpu.VMEM((PLACES, 8, 128), F32),
            pltpu.VMEM((2, CHUNKS, CHUNK, 256), BF16),
            pltpu.VMEM((CHUNKS + 1, CHUNK, ROWS), BF16),
            pltpu.VMEM((CHUNKS + 1, CHUNK, ROWS), BF16),
            pltpu.VMEM((NZ, 8, 384), F32),
            pltpu.VMEM((NZ, 8, 384), F32),
            pltpu.VMEM((2, NZ, NY, 8, 128), F32),
            pltpu.VMEM((NZ, 8, 128), F32),
            pltpu.VMEM((NZ, 8, 128), F32),
            pltpu.SemaphoreType.DMA((10,)),
            pltpu.SemaphoreType.DMA((2, CHUNKS)),
            pltpu.SemaphoreType.DMA((2, 1 + PARTS)),
            pltpu.SemaphoreType.DMA((2, 3)),
            pltpu.SemaphoreType.DMA((PARTS,)),
            pltpu.SemaphoreType.DMA((2,)),
            pltpu.SemaphoreType.DMA((2, 3)),
        ],
        compiler_params=pltpu.CompilerParams(
            collective_id=0, has_side_effects=True, vmem_limit_bytes=60 * 2**20
        ),
        name="ladder",
    )(
        block_starts,
        singles,
        pair_list,
        row_pairs.transpose(0, 2, 1),
        col_pairs.transpose(0, 2, 1),
        t2_slab,
        w_hole,
        driver,
        occ_energy.reshape(1, OCC),
        vir_energy.reshape(1, VIRT),
        t2_packed.T.reshape(CHUNKS, CHUNK, ROWS),
        w_packed.reshape(CHUNKS, CHUNK, COLS),
    )


def solution(mesh):
    in_specs = (
        P(None, ("virt", "rep")),
        P(("virt", "rep"), None),
        P(None, ("virt", "rep")),
        P(),
        P(),
        P(),
        P(None, "rep", None),
        P(None, "virt", "rep"),
        P(None, "virt", None),
        P(None, "virt", "rep"),
        P(),
        P(),
    )
    out_specs = P(None, "virt", "rep")
    return jax.shard_map(body, mesh=mesh, in_specs=in_specs, out_specs=out_specs, check_vma=False)
```
